32 devices in a mesh: expert: 4 (over y, x), context: 4 (over z), tensor: 2 (over core).
Axes of the slice: x: 2, y: 2, z: 4, core: 2. Of those that a mesh axis runs over, the one named last changes fastest.
Arguments:
- queries: bfloat16 [2048, 2048], P(('expert', 'context'), 'tensor'), may hold values from -6 to 6
- key_input: bfloat16 [2048, 2048], P(('expert', 'context'), 'tensor'), may hold values from -6 to 6
- value_input: bfloat16 [2048, 2048], P(('expert', 'context'), 'tensor'), may hold values from -6 to 6
- residual: bfloat16 [2048, 2048], P(('expert', 'context'), 'tensor'), may hold values from -40 to 40
- grad_output: bfloat16 [2048, 2048], P(('expert', 'context'), 'tensor'), may hold values from -6 to 6
- expert_of: int32 [2048, 1], P(('expert', 'context')), may hold values from 0 to 7; in each aligned block of 128 rows (0 to 127, 128 to 255, ...) at most 18 rows name the same one
- gate_weight: bfloat16 [8, 2048, 4096], P(('expert', 'tensor'), None, 'context'), may hold values from -0.125 to 0.125
- up_weight: bfloat16 [8, 2048, 4096], P(('expert', 'tensor'), None, 'context'), may hold values from -0.125 to 0.125
- down_weight: bfloat16 [8, 4096, 2048], P(('expert', 'tensor'), 'context'), may hold values from -0.09375 to 0.09375
Outputs:
- grad_queries: bfloat16 [2048, 2048], P(('expert', 'context'), 'tensor')
- grad_keys: bfloat16 [2048, 2048], P(('expert', 'context'), 'tensor')
- grad_values: bfloat16 [2048, 2048], P(('expert', 'context'), 'tensor')
- grad_residual: bfloat16 [2048, 2048], P(('expert', 'context'), 'tensor')
- grad_gate: bfloat16 [8, 2048, 4096], P(('expert', 'tensor'), None, 'context')
- grad_up: bfloat16 [8, 2048, 4096], P(('expert', 'tensor'), None, 'context')
- grad_down: bfloat16 [8, 4096, 2048], P(('expert', 'tensor'), 'context')
The draws below stay inside these ranges and needn't reach their ends.
Inputs may be any that keep to these rules, and one draw needn't show every extreme that they name: `expert_of`: in each aligned block of 128 rows (the rows of one device) no expert is named by more than 18 rows, and 18 is reached in some block.
All inputs are finite; a program needn't handle non-finite values.
Results may differ from the reference program's by a relative error of at most 0.011.
Values may be sent and summed in bfloat16 or wider, within the bound.
A program may use at most 192 MiB of HBM per device.

```python
import math
import jax
import jax.numpy as jnp
import numpy as np
from jax import lax

TOK_DEV = 128
H = 16
HD = 128
FF = 4096
D = 2048
SEQ = 512
TOKENS = 2048
EXPERTS = 8
CAP = 18
N_EXPERT = 4
N_CONTEXT = 4


def paired_rows(key, rate):
    pieces = jax.random.split(key, 5)
    query_rows = jnp.clip(jax.random.normal(pieces[0], (TOKENS, D), jnp.float32), -6.0, 6.0)
    key_rows = jnp.clip(jax.random.normal(pieces[1], (TOKENS, D), jnp.float32), -6.0, 6.0)
    position = jnp.arange(TOKENS, dtype=jnp.int32) % SEQ
    chosen = (jax.random.uniform(pieces[2], (TOKENS,), jnp.float32) < rate) & (position > 0)
    pattern = jnp.where(jax.random.uniform(pieces[3], (TOKENS, D), jnp.float32) < 0.5, -1.0, 1.0)
    levels = jnp.array([3.0, 4.5, 6.0], jnp.float32)
    strength = levels[jax.random.randint(pieces[4], (TOKENS,), 0, 3)]
    aligned = pattern * strength[:, None]
    query_rows = jnp.where(chosen[:, None], aligned, query_rows)
    key_rows = jnp.where(chosen[:, None], aligned, key_rows)
    damped = aligned * (1.0 - 2.0 / (strength * strength * math.sqrt(HD)))[:, None]
    following = jnp.roll(chosen, -1)
    key_rows = jnp.where(following[:, None], jnp.roll(damped, -1, axis=0), key_rows)
    return (query_rows, key_rows)


def draw_queries(key, part):
    rate = 0.0
    query_rows, key_rows = paired_rows(key, rate)
    return query_rows.astype(jnp.bfloat16)


def draw_key_input(key, part):
    rate = 0.0
    query_rows, key_rows = paired_rows(key, rate)
    return key_rows.astype(jnp.bfloat16)


def draw_residual(key, part):
    key = jax.random.fold_in(key, 29)
    pieces = jax.random.split(key, 3)
    row_scale = jnp.exp(jax.random.uniform(pieces[1], (TOKENS, 1), jnp.float32, math.log(0.3), math.log(3.0)))
    column_scale = jnp.exp(jax.random.uniform(pieces[2], (1, D), jnp.float32, math.log(0.3), math.log(3.0)))
    raw_values = jax.random.normal(pieces[0], (TOKENS, D), jnp.float32)
    return jnp.clip(raw_values * row_scale * column_scale, -40.0, 40.0).astype(jnp.bfloat16)


def block_levels(rng, shape, cuts, low, largest):
    def one(dim, blocks):
        draws = jax.random.uniform(jax.random.fold_in(jax.random.fold_in(rng, 6), dim), (blocks,), jnp.float32, low / len(cuts), largest / len(cuts))
        return jnp.repeat(jnp.exp(draws), shape[dim] // blocks).reshape((-1,) + (1,) * (len(shape) - dim - 1))

    gain = one(*cuts[0])
    for cut in cuts[1:]:
        gain = gain * one(*cut)
    return gain


def assign_block(rng, own, number, rows, number_of, top, most, slope):
    sequence = jax.random.permutation(rng, number_of)
    heavy_load, usual = load_shares(number_of, rows * top, most, slope, True), load_shares(number_of, rows * top, most, slope, False)
    places = jnp.arange(number_of)

    def named(tallies, offset_by):
        used = int((tallies > 0).sum())
        fixed = max(1, used // 4)
        passed = fixed + (places - fixed + offset_by * (used - fixed)) % max(1, number_of - fixed)
        return jnp.zeros((number_of,), jnp.int32).at[sequence[jnp.where(places < fixed, places, passed)]].set(jnp.asarray(tallies, jnp.int32))

    tallies = jnp.where(number % 4 == 0, named(heavy_load, number // 4), named(usual, number - number // 4 - 1))
    mixed = jax.random.permutation(jax.random.fold_in(own, 3), number_of)
    source_of, sink = mixed[0:number_of // 2 * 2:2], mixed[1:number_of // 2 * 2:2]
    room = jnp.minimum(tallies[source_of] - 1, most - tallies[sink]) // 2
    room = jnp.where((source_of == sequence[0]) | (sink == sequence[0]) | (tallies[sink] == 0), 0, jnp.maximum(room, 0))
    passed = jax.random.randint(jax.random.fold_in(own, 4), (number_of // 2,), 0, 1 << 20) % (room + 1)
    tallies = tallies.at[source_of].add(-passed).at[sink].add(passed)
    items = jnp.searchsorted(jnp.cumsum(tallies), jnp.arange(rows * top), side="right").astype(jnp.int32)
    grid = items.reshape(top, rows).T
    grid = grid[jax.random.permutation(jax.random.fold_in(own, 1), rows)]
    offset_by = jax.random.randint(jax.random.fold_in(own, 2), (rows, 1), 0, top)
    return jnp.take_along_axis(grid, (jnp.arange(top)[None, :] + offset_by) % top, axis=1)


def load_shares(number_of, total, most, skew, full):
    weights = [(1 << 20) // math.isqrt(rank ** skew) + 1 for rank in range(1, number_of + 1)]
    largest = most if full else min(most, max(-(-total // number_of), total * weights[0] // sum(weights)))
    least = 1 if total - largest >= number_of - 1 else 0
    given, spare = [largest] + [least] * (number_of - 1), total - largest - least * (number_of - 1)
    while spare > 0:
        movable = [i for i in range(1, number_of) if given[i] < largest] or [i for i in range(1, number_of) if given[i] < most]
        whole, budget = sum([weights[i] for i in movable]), spare
        for i in movable:
            extra = min(most - given[i], max(1, budget * weights[i] // whole), spare)
            given[i] = given[i] + extra
            spare = spare - extra
    return np.array(given)


def bell_draw(key, dims, deviation, most, cuts=(), kind=jnp.bfloat16):
    result = deviation * jax.random.normal(key, dims, jnp.float32)
    if cuts:
        result = result * block_levels(key, dims, cuts, -0.22, 0.18)
    return jnp.clip(result, -most, most).astype(kind)


def setup_inputs(seed: int = 0) -> dict:
    splits = jax.random.split(jax.random.key(seed), 10)
    queries = draw_queries(jax.random.fold_in(splits[9], 71), 0)
    key_input = draw_key_input(jax.random.fold_in(splits[9], 71), 0)
    value_input = bell_draw(splits[2], (TOKENS, D), 1.0, 6.0, ((0, 16), (1, 2)))
    residual = draw_residual(jax.random.fold_in(splits[9], 71), 0)
    grad_output = bell_draw(splits[4], (TOKENS, D), 1.0, 6.0, ((0, 16), (1, 2)))
    expert_of_keys = jax.random.split(jax.random.fold_in(splits[5], 1), TOKENS // TOK_DEV)
    expert_of_turns = jax.random.permutation(jax.random.fold_in(splits[5], 3), TOKENS // TOK_DEV)
    expert_of = jax.vmap(lambda own, number: assign_block(jax.random.fold_in(splits[5], 2), own, number, TOK_DEV, EXPERTS, 1, CAP, 1))(expert_of_keys, expert_of_turns).reshape((TOKENS, 1))
    gate_weight = bell_draw(splits[6], (EXPERTS, D, FF), D ** -0.5, 0.125, ((0, 8), (2, 4)))
    up_weight = bell_draw(splits[7], (EXPERTS, D, FF), D ** -0.5, 0.125, ((0, 8), (2, 4)))
    down_weight = bell_draw(splits[8], (EXPERTS, FF, D), FF ** -0.5, 0.09375, ((0, 8), (1, 4)))
    return dict(queries=queries, key_input=key_input, value_input=value_input, residual=residual, grad_output=grad_output, expert_of=expert_of, gate_weight=gate_weight, up_weight=up_weight, down_weight=down_weight)


EPSILON = 1e-06

def widen(array):
    return lax.optimization_barrier(array).astype(jnp.float32)

def sequence_probs(query_seq, key_seq):
    length = query_seq.shape[0]
    query_f = query_seq.astype(jnp.float32).reshape(length, H, HD)
    key_f = key_seq.astype(jnp.float32).reshape(length, H, HD)
    scores = jnp.einsum('qhd,khd->hqk', query_f, key_f) * HD ** (-0.5)
    position = jnp.arange(length, dtype=jnp.int32)
    causal = position[None, :] <= position[:, None]
    scores = jnp.where(causal[None], scores, -jnp.inf)
    row_max = lax.optimization_barrier(jnp.max(scores, axis=-1, keepdims=True))
    shifted = jnp.exp(scores - row_max)
    row_total = lax.optimization_barrier(jnp.sum(shifted, axis=-1, keepdims=True))
    return (shifted / row_total).astype(jnp.bfloat16)

def sequence_forward(items):
    query_seq, key_seq, value_seq = items
    length = query_seq.shape[0]
    attn_probs = sequence_probs(query_seq, key_seq)
    value_f = value_seq.astype(jnp.float32).reshape(length, H, HD)
    attn = jnp.einsum('hqk,khd->qhd', widen(attn_probs), value_f)
    return attn.reshape(length, H * HD).astype(jnp.bfloat16)

def sequence_backward(items):
    query_seq, key_seq, value_seq, grad_seq = items
    length = query_seq.shape[0]
    attn_probs = sequence_probs(query_seq, key_seq)
    query_f = query_seq.astype(jnp.float32).reshape(length, H, HD)
    key_f = key_seq.astype(jnp.float32).reshape(length, H, HD)
    value_f = value_seq.astype(jnp.float32).reshape(length, H, HD)
    grad_f = widen(grad_seq).reshape(length, H, HD)
    probs_f = widen(attn_probs)
    grad_probs = jnp.einsum('qhd,khd->hqk', grad_f, value_f)
    row_dot = lax.optimization_barrier(jnp.sum(probs_f * grad_probs, axis=-1, keepdims=True))
    grad_scores = (probs_f * (grad_probs - row_dot) * HD ** (-0.5)).astype(jnp.bfloat16)
    scores_f = widen(grad_scores)
    grad_query = jnp.einsum('hqk,khd->qhd', scores_f, key_f).reshape(length, H * HD)
    grad_key = jnp.einsum('hqk,qhd->khd', scores_f, query_f).reshape(length, H * HD)
    grad_value = jnp.einsum('hqk,qhd->khd', probs_f, grad_f).reshape(length, H * HD)
    return (grad_query.astype(jnp.bfloat16), grad_key.astype(jnp.bfloat16), grad_value.astype(jnp.bfloat16))

def expert_pass(items):
    rows_normed, rows_grad, gate_w, up_w, down_w = items
    gate = jnp.dot(rows_normed, gate_w, preferred_element_type=jnp.float32)
    up_val = jnp.dot(rows_normed, up_w, preferred_element_type=jnp.float32)
    sig = jax.nn.sigmoid(gate)
    activation = (gate * sig * up_val).astype(jnp.bfloat16)
    grad_act = jnp.dot(rows_grad, down_w.T, preferred_element_type=jnp.float32)
    grad_gate_rows = (grad_act * up_val * sig * (1.0 + gate * (1.0 - sig))).astype(jnp.bfloat16)
    grad_up_rows = (grad_act * gate * sig).astype(jnp.bfloat16)
    grad_down_w = jnp.dot(activation.T, rows_grad, preferred_element_type=jnp.float32).astype(jnp.bfloat16)
    grad_gate_w = jnp.dot(rows_normed.T, grad_gate_rows, preferred_element_type=jnp.float32).astype(jnp.bfloat16)
    grad_up_w = jnp.dot(rows_normed.T, grad_up_rows, preferred_element_type=jnp.float32).astype(jnp.bfloat16)
    grad_normed = jnp.dot(grad_gate_rows, gate_w.T, preferred_element_type=jnp.float32)
    grad_normed = grad_normed + jnp.dot(grad_up_rows, up_w.T, preferred_element_type=jnp.float32)
    return (grad_gate_w, grad_up_w, grad_down_w, grad_normed)

def reference(queries, key_input, value_input, residual, grad_output, expert_of, gate_weight, up_weight, down_weight):
    features = H * HD
    shape3 = (N_EXPERT, SEQ, features)
    attn = lax.map(sequence_forward, (queries.reshape(shape3), key_input.reshape(shape3), value_input.reshape(shape3)))
    attn = attn.reshape(TOKENS, features)
    state = residual.astype(jnp.float32) + widen(attn)
    inv_rms = 1.0 / jnp.sqrt(lax.optimization_barrier(jnp.mean(state * state, axis=-1, keepdims=True)) + EPSILON)
    normed_exact = state * inv_rms
    normed = normed_exact.astype(jnp.bfloat16)
    expert_ids = expert_of[:, 0].astype(jnp.int32)
    token_index = jnp.arange(TOKENS, dtype=jnp.int32)
    block = (token_index // TOK_DEV).astype(jnp.int32)
    onehot = (expert_ids[:, None] == jnp.arange(EXPERTS, dtype=jnp.int32)[None, :]).astype(jnp.int32)
    blocked = onehot.reshape(TOKENS // TOK_DEV, TOK_DEV, EXPERTS)
    earlier = jnp.cumsum(blocked, axis=1) - blocked
    slot_of = lax.optimization_barrier(jnp.sum((earlier * blocked).reshape(TOKENS, EXPERTS), axis=1)).astype(jnp.int32)
    source = block // N_CONTEXT
    context = block % N_CONTEXT
    group = N_CONTEXT * N_EXPERT * CAP
    spot = (((expert_ids * N_CONTEXT + context) * N_EXPERT + source) * CAP + slot_of).astype(jnp.int32)
    normed_buf = jnp.zeros((EXPERTS * group, features), normed.dtype).at[spot].set(normed)
    grad_buf = jnp.zeros((EXPERTS * group, features), grad_output.dtype).at[spot].set(grad_output)
    normed_buf = normed_buf.reshape(EXPERTS, group, features)
    grad_buf = grad_buf.reshape(EXPERTS, group, features)
    grad_gate, grad_up, grad_down, grad_normed_buf = lax.map(expert_pass, (normed_buf, grad_buf, gate_weight, up_weight, down_weight))
    grad_normed = grad_normed_buf.reshape(EXPERTS * group, features)[spot]
    inner = lax.optimization_barrier(jnp.mean(normed_exact * grad_normed, axis=-1, keepdims=True))
    grad_state = grad_output.astype(jnp.float32) + inv_rms * (grad_normed - normed_exact * inner)
    grad_residual = grad_state.astype(jnp.bfloat16)
    grad_q, grad_k, grad_v = lax.map(sequence_backward, (queries.reshape(shape3), key_input.reshape(shape3), value_input.reshape(shape3), grad_residual.reshape(shape3)))
    return (grad_q.reshape(TOKENS, features), grad_k.reshape(TOKENS, features), grad_v.reshape(TOKENS, features), grad_residual, grad_gate, grad_up, grad_down)
```

```python
import functools

import jax
import jax.numpy as jnp
from jax import lax
from jax.experimental import pallas as pl
from jax.experimental.pallas import tpu as pltpu
from jax.sharding import PartitionSpec as P

HD = 128
MESH = pl.DeviceIdType.MESH


EPSILON = 1e-06


def widen(array):
    return lax.optimization_barrier(array).astype(jnp.float32)


def masked_scores(query_heads, key_heads, query_start, score_scale):
    scores = (
        jnp.einsum("qhd,khd->hqk", query_heads, key_heads, preferred_element_type=jnp.float32)
        * score_scale
    )
    query_pos = query_start + jnp.arange(query_heads.shape[0], dtype=jnp.int32)
    key_pos = jnp.arange(key_heads.shape[0], dtype=jnp.int32)
    causal = key_pos[None, :] <= query_pos[:, None]
    return jnp.where(causal[None], scores, -jnp.inf)


def on_device(
    queries,
    key_input,
    value_input,
    residual,
    grad_output,
    expert_of,
    gate_weight,
    up_weight,
    down_weight,
):
    row_count = queries.shape[0]
    head_count = queries.shape[1] // HD
    n_expert = lax.axis_size("expert")
    n_tensor = lax.axis_size("tensor")
    features = queries.shape[1] * n_tensor
    score_scale = HD ** (-0.5)
    own_start = lax.axis_index("context") * row_count
    own_parity = lax.axis_index("tensor")
    all_keys, all_values = (
        lax.all_gather(key_input, "context", axis=0, tiled=True),
        lax.all_gather(value_input, "context", axis=0, tiled=True),
    )
    length = all_keys.shape[0]
    query_heads = queries.reshape(row_count, head_count, HD)
    key_heads = all_keys.reshape(length, head_count, HD)
    value_heads = all_values.reshape(length, head_count, HD)
    scores = masked_scores(query_heads, key_heads, own_start, score_scale)
    row_max = jnp.max(scores, axis=-1, keepdims=True)
    shifted = jnp.exp(scores - row_max)
    row_total = jnp.sum(shifted, axis=-1, keepdims=True)
    attn_probs = (shifted / row_total).astype(jnp.bfloat16)
    attn = jnp.einsum("hqk,khd->qhd", attn_probs, value_heads, preferred_element_type=jnp.float32)
    attn = attn.astype(jnp.bfloat16).reshape(row_count, -1)
    state = residual.astype(jnp.float32) + widen(attn)
    total_sq = lax.psum(jnp.sum(state * state, axis=-1), "tensor")
    inv_rms = (1.0 / jnp.sqrt(total_sq / features + EPSILON))[:, None]
    normed_exact = state * inv_rms
    normed = normed_exact.astype(jnp.bfloat16)
    n_all = n_expert * n_tensor
    capacity = row_count // n_all + max(1, row_count // (8 * n_all))
    expert_ids = expert_of[:, 0]
    onehot = (expert_ids[:, None] == jnp.arange(n_all, dtype=jnp.int32)[None, :]).astype(jnp.int32)
    earlier = jnp.cumsum(onehot, axis=0) - onehot
    slot_of = jnp.sum(earlier * onehot, axis=1)
    mine = expert_ids % n_tensor == own_parity
    target = jnp.where(mine, expert_ids // n_tensor * capacity + slot_of, n_expert * capacity)
    placing = (target[None, :] == jnp.arange(n_expert * capacity, dtype=jnp.int32)[:, None]).astype(
        jnp.bfloat16
    )
    full_normed, full_grad = (
        lax.all_gather(normed, "tensor", axis=1, tiled=True),
        lax.all_gather(grad_output, "tensor", axis=1, tiled=True),
    )
    send_normed = jnp.dot(placing, full_normed, preferred_element_type=jnp.float32).astype(
        jnp.bfloat16
    )
    send_grad = jnp.dot(placing, full_grad, preferred_element_type=jnp.float32).astype(jnp.bfloat16)
    send_normed = send_normed.reshape(n_expert, capacity, -1)
    send_grad = send_grad.reshape(n_expert, capacity, -1)
    got_normed, got_grad = (
        lax.all_to_all(send_normed, "expert", split_axis=0, concat_axis=0, tiled=True),
        lax.all_to_all(send_grad, "expert", split_axis=0, concat_axis=0, tiled=True),
    )
    routed_normed, routed_grad = (
        lax.all_gather(got_normed[None], "context", axis=0, tiled=True),
        lax.all_gather(got_grad[None], "context", axis=0, tiled=True),
    )
    routed_normed = routed_normed.reshape(-1, features)
    routed_grad = routed_grad.reshape(-1, features)
    gate_local = gate_weight[0]
    up_local = up_weight[0]
    down_local = down_weight[0]
    gate = jnp.dot(routed_normed, gate_local, preferred_element_type=jnp.float32)
    up_value = jnp.dot(routed_normed, up_local, preferred_element_type=jnp.float32)
    sigmoid_gate = jax.nn.sigmoid(gate)
    activation = (gate * sigmoid_gate * up_value).astype(jnp.bfloat16)
    grad_act = jnp.einsum("rd,fd->rf", routed_grad, down_local, preferred_element_type=jnp.float32)
    grad_gate_rows = (
        grad_act * up_value * sigmoid_gate * (1.0 + gate * (1.0 - sigmoid_gate))
    ).astype(jnp.bfloat16)
    grad_up_rows = (grad_act * gate * sigmoid_gate).astype(jnp.bfloat16)
    grad_down = jnp.dot(activation.T, routed_grad, preferred_element_type=jnp.float32).astype(
        jnp.bfloat16
    )[None]
    grad_gate = jnp.dot(routed_normed.T, grad_gate_rows, preferred_element_type=jnp.float32).astype(
        jnp.bfloat16
    )[None]
    grad_up = jnp.dot(routed_normed.T, grad_up_rows, preferred_element_type=jnp.float32).astype(
        jnp.bfloat16
    )[None]
    term = jnp.einsum("rf,df->rd", grad_gate_rows, gate_local, preferred_element_type=jnp.float32)
    summed_rows = lax.psum_scatter(
        term + jnp.einsum("rf,df->rd", grad_up_rows, up_local, preferred_element_type=jnp.float32),
        "context",
        scatter_dimension=0,
        tiled=True,
    )
    returned = lax.all_to_all(
        summed_rows.reshape(n_expert, capacity, -1),
        "expert",
        split_axis=0,
        concat_axis=0,
        tiled=True,
    )
    padded = jnp.concatenate(
        [returned.reshape(n_expert * capacity, -1), jnp.zeros((1, features), jnp.float32)], axis=0
    )
    full_grad_normed = jnp.take(padded, target, axis=0)
    grad_normed = lax.psum_scatter(full_grad_normed, "tensor", scatter_dimension=1, tiled=True)
    inner_sum = lax.psum(jnp.sum(normed_exact * grad_normed, axis=-1), "tensor")
    grad_state = grad_output.astype(jnp.float32) + inv_rms * (
        grad_normed - normed_exact * (inner_sum / features)[:, None]
    )
    grad_residual = grad_state.astype(jnp.bfloat16)
    grad_heads = grad_residual.reshape(row_count, head_count, HD)
    grad_probs = jnp.einsum(
        "qhd,khd->hqk", grad_heads, value_heads, preferred_element_type=jnp.float32
    )
    probs_exact = widen(attn_probs)
    row_dot = jnp.sum(probs_exact * grad_probs, axis=-1, keepdims=True)
    grad_scores = (probs_exact * (grad_probs - row_dot) * score_scale).astype(jnp.bfloat16)
    grad_queries = jnp.einsum(
        "hqk,khd->qhd", grad_scores, key_heads, preferred_element_type=jnp.float32
    )
    grad_queries = grad_queries.astype(jnp.bfloat16).reshape(row_count, -1)
    key_part = jnp.einsum(
        "hqk,qhd->khd", grad_scores, query_heads, preferred_element_type=jnp.float32
    )
    value_part = jnp.einsum(
        "hqk,qhd->khd", attn_probs, grad_heads, preferred_element_type=jnp.float32
    )
    combined = lax.psum_scatter(
        jnp.concatenate(
            [
                key_part.reshape(lax.axis_size("context") * row_count, -1),
                value_part.reshape(lax.axis_size("context") * row_count, -1),
            ],
            axis=1,
        ),
        "context",
        scatter_dimension=0,
        tiled=True,
    )
    split_at = combined.shape[1] // 2
    grad_keys = combined[:, :split_at].astype(jnp.bfloat16)
    grad_values = combined[:, split_at:].astype(jnp.bfloat16)
    return (grad_queries, grad_keys, grad_values, grad_residual, grad_gate, grad_up, grad_down)


def remote(src, dst, send_sem, recv_sem, target):
    return pltpu.make_async_remote_copy(
        src_ref=src,
        dst_ref=dst,
        send_sem=send_sem,
        recv_sem=recv_sem,
        device_id=target,
        device_id_type=MESH,
    )


def position():
    return lax.axis_index("expert"), lax.axis_index("context"), lax.axis_index("tensor")


def partner(step, sizes):
    n_expert, n_context, n_tensor = sizes
    own_expert, own_context, own_tensor = position()
    own = (own_expert * n_context + own_context) * n_tensor + own_tensor
    other = lax.rem(own + step, n_expert * n_context * n_tensor)
    return (
        other // (n_context * n_tensor),
        lax.rem(other // n_tensor, n_context),
        lax.rem(other, n_tensor),
    )


def greet_all(sizes):
    n_devices = sizes[0] * sizes[1] * sizes[2]
    barrier = pltpu.get_barrier_semaphore()

    @pl.loop(1, n_devices)
    def _(step):
        pl.semaphore_signal(barrier, inc=1, device_id=partner(step, sizes), device_id_type=MESH)

    return barrier, n_devices - 1


def aligned(start, size):
    return pl.ds(pl.multiple_of(start, size), size)


def dot(left, right, left_dim=1, right_dim=0):
    return lax.dot_general(
        left, right, (((left_dim,), (right_dim,)), ((), ())), preferred_element_type=jnp.float32
    )


def forward_kernel(sizes, rows, slots, ids_ref, q_ref, k_ref, v_ref, r_ref, g_ref,
                   x_out, g_out, place_ref, probs_ref, qh, kh, vh, gh,
                   rh, ids_all, state, x_send, g_send,
                   in_send, in_recv, out_send, out_recv):
    n_expert, n_context, n_tensor = sizes
    n_devices = n_expert * n_context * n_tensor
    n_all = n_expert * n_tensor
    own_expert, own_context, own_tensor = position()
    width = qh.shape[1]
    length = qh.shape[0]
    barrier, count = greet_all(sizes)
    pl.semaphore_wait(barrier, count)
    moves = [(g_ref, gh), (q_ref, qh), (k_ref, kh), (v_ref, vh), (r_ref, rh)]

    def in_copy(number, step):
        target = lax.rem(own_context + step, n_context)
        if number == len(moves):
            src, dst = ids_ref, ids_all.at[own_context]
        else:
            src = moves[number][0].at[:, aligned(target * width, width)]
            dst = moves[number][1].at[aligned(own_context * rows, rows), :]
        return remote(src, dst, in_send.at[number, step], in_recv.at[number, step],
                      (own_expert, target, own_tensor))

    for number in [len(moves), 0, 1, 2, 3, 4]:
        for step in range(1, n_context):
            in_copy(number, step).start()
    ids_all[own_context] = ids_ref[...]
    for src, dst in moves:
        dst[aligned(own_context * rows, rows), :] = src[:, aligned(own_context * width, width)]

    def arrived(number):
        for step in range(1, n_context):
            in_copy(number, step).wait_recv()

    def out_copy(kind, step):
        src, dst = ((g_send, g_out), (x_send, x_out))[kind]
        expert, context, tensor = partner(step, sizes)
        return remote(
            src.at[aligned((expert * n_tensor + tensor) * slots, slots), :],
            dst.at[aligned(own_expert * slots, slots),
                   aligned((own_tensor * n_context + own_context) * width, width)],
            out_send.at[kind, step], out_recv.at[kind, step], (expert, context, tensor))

    def dispatch(kind, send, out, source):
        for e in range(n_all):
            send[e * slots:(e + 1) * slots, :] = dot(
                place_ref[e * slots:(e + 1) * slots, :], source[...]).astype(jnp.bfloat16)

        @pl.loop(1, n_devices)
        def _(step):
            out_copy(kind, step).start()

        out[aligned(own_expert * slots, slots),
            aligned((own_tensor * n_context + own_context) * width, width)] = send[
                aligned((own_expert * n_tensor + own_tensor) * slots, slots), :]

    arrived(len(moves))
    named = lax.broadcasted_iota(jnp.int32, (n_all, rows), 0)
    onehot = jnp.concatenate(
        [(ids_all[c] == named).astype(jnp.float32) for c in range(n_context)], axis=1)
    before = (lax.broadcasted_iota(jnp.int32, (length, length), 0)
              < lax.broadcasted_iota(jnp.int32, (length, length), 1))
    rank = dot(onehot.astype(jnp.bfloat16), before.astype(jnp.float32).astype(jnp.bfloat16))
    rank = jnp.where(onehot > 0.5, rank, -1.0)
    slot = lax.broadcasted_iota(jnp.int32, (slots, length), 0).astype(jnp.float32)
    for e in range(n_all):
        place_ref[e * slots:(e + 1) * slots, :] = (
            (rank[e:e + 1, :] == slot).astype(jnp.float32).astype(jnp.bfloat16))
    arrived(0)
    dispatch(0, g_send, g_out, gh)
    for number in (1, 2, 3, 4):
        arrived(number)
    heads = width // HD
    for h in range(heads):
        cols = slice(h * HD, (h + 1) * HD)
        for c in range(n_context):
            seen = (c + 1) * rows
            block = slice(c * rows, seen)
            scores = dot(qh[block, cols], kh[:seen, cols], 1, 1) * HD ** (-0.5)
            query = c * rows + lax.broadcasted_iota(jnp.int32, (rows, seen), 0)
            key = lax.broadcasted_iota(jnp.int32, (rows, seen), 1)
            scores = jnp.where(key <= query, scores, -jnp.inf)
            shifted = jnp.exp(scores - jnp.max(scores, axis=1, keepdims=True))
            probs = (shifted / jnp.sum(shifted, axis=1, keepdims=True)).astype(jnp.bfloat16)
            probs_ref[h, block, :seen] = probs
            attn = dot(probs, vh[:seen, cols]).astype(jnp.bfloat16).astype(jnp.float32)
            state[block, cols] = (rh[block, cols].astype(jnp.float32) + attn).astype(jnp.bfloat16)
    dispatch(1, x_send, x_out, state)

    @pl.loop(1, n_devices)
    def _(step):
        for kind in (0, 1):
            out_copy(kind, step).wait()

    for number in range(len(moves) + 1):
        for step in range(1, n_context):
            in_copy(number, step).wait_send()


def expert_kernel(sizes, slots, tile, x_ref, g_ref, gate_hbm, up_hbm, down_hbm,
                  back, grad_gate_hbm, grad_up_hbm, grad_down_hbm,
                  gate_w, up_w, down_w, act, dgate, dup, inv_ref, inner_ref, r_send,
                  gate_out, up_out, down_out, load_sem, store_sem, send_sem, recv_sem):
    n_expert, n_context, n_tensor = sizes
    n_devices = n_expert * n_context * n_tensor
    n_all = n_expert * n_tensor
    own_expert, own_context, own_tensor = position()
    features, hidden = gate_w.shape
    tiles = hidden // tile
    width = r_send.shape[2]
    pieces = features // width

    def load(number, f):
        part = aligned(f * tile, tile)
        src, dst = ((gate_hbm.at[0, :, part], gate_w.at[:, part]),
                    (up_hbm.at[0, :, part], up_w.at[:, part]),
                    (down_hbm.at[0, part, :], down_w.at[part, :]))[number]
        return pltpu.make_async_copy(src, dst, load_sem.at[number, f])

    for f in range(tiles):
        for number in range(3):
            load(number, f).start()
    barrier, count = greet_all(sizes)
    x32 = x_ref[...].astype(jnp.float32)
    inv_ref[...] = 1.0 / jnp.sqrt(
        jnp.sum(x32 * x32, axis=1, keepdims=True) / features + EPSILON)
    inner_ref[...] = jnp.zeros_like(inner_ref)
    for f in range(tiles):
        part = slice(f * tile, (f + 1) * tile)
        for number in range(3):
            load(number, f).wait()
        inv = inv_ref[...]
        gate = dot(x_ref[...], gate_w[:, part]) * inv
        up = dot(x_ref[...], up_w[:, part]) * inv
        grad_act = dot(g_ref[...], down_w[part, :], 1, 1)
        sig = 1.0 / (1.0 + jnp.exp(-gate))
        grad_up = grad_act * gate * sig
        grad_gate = grad_act * up * sig * (1.0 + gate * (1.0 - sig))
        act[:, part] = (gate * sig * up).astype(jnp.bfloat16)
        inner_ref[...] += jnp.sum(grad_gate * gate + grad_up * up, axis=1, keepdims=True)
        dgate[:, part] = (grad_gate * inv).astype(jnp.bfloat16)
        dup[:, part] = (grad_up * inv).astype(jnp.bfloat16)
    inner_ref[...] = inner_ref[...] * inv_ref[...] * inv_ref[...] / features
    pl.semaphore_wait(barrier, count)

    def piece_copy(piece, seq):
        tensor, context = piece // n_context, lax.rem(piece, n_context)
        return remote(
            r_send.at[piece, aligned(seq * slots, slots), :],
            back.at[own_context, aligned((own_expert * n_tensor + own_tensor) * slots, slots), :],
            send_sem.at[piece, seq],
            recv_sem.at[own_context, own_expert * n_tensor + own_tensor],
            (seq, context, tensor))

    def is_own(piece, seq):
        return (piece == own_tensor * n_context + own_context) & (seq == own_expert)

    @pl.loop(0, pieces)
    def _(turn):
        piece = lax.rem(own_tensor * n_context + own_context + 1 + turn, pieces)
        part = aligned(piece * width, width)
        grad = dot(dgate[...], gate_w[part, :], 1, 1) + dot(dup[...], up_w[part, :], 1, 1)
        grad = grad - x_ref[:, part].astype(jnp.float32) * inner_ref[...]
        r_send[piece] = grad.astype(jnp.bfloat16)

        @pl.loop(0, n_expert)
        def _(seq):
            @pl.when(jnp.logical_not(is_own(piece, seq)))
            def _():
                piece_copy(piece, seq).start()

    back[own_context, aligned((own_expert * n_tensor + own_tensor) * slots, slots), :] = r_send[
        own_tensor * n_context + own_context, aligned(own_expert * slots, slots), :]

    def store(number, f):
        part = aligned(f * tile, tile)
        src, dst = ((gate_out.at[:, part], grad_gate_hbm.at[0, :, part]),
                    (up_out.at[:, part], grad_up_hbm.at[0, :, part]),
                    (down_out.at[part, :], grad_down_hbm.at[0, part, :]))[number]
        return pltpu.make_async_copy(src, dst, store_sem.at[number, f])

    for f in range(tiles):
        part = slice(f * tile, (f + 1) * tile)
        down_out[part, :] = dot(act[:, part], g_ref[...], 0, 0).astype(jnp.bfloat16)
        store(2, f).start()
        gate_out[:, part] = dot(x_ref[...], dgate[:, part], 0, 0).astype(jnp.bfloat16)
        store(0, f).start()
        up_out[:, part] = dot(x_ref[...], dup[:, part], 0, 0).astype(jnp.bfloat16)
        store(1, f).start()

    @pl.loop(0, pieces)
    def _(piece):
        @pl.loop(0, n_expert)
        def _(seq):
            @pl.when(jnp.logical_not(is_own(piece, seq)))
            def _():
                piece_copy(piece, seq).wait_send()

    @pl.loop(0, n_context)
    def _(context):
        @pl.loop(0, n_all)
        def _(expert):
            @pl.when(jnp.logical_not(
                (context == own_context) & (expert == own_expert * n_tensor + own_tensor)))
            def _():
                part = back.at[context, aligned(expert * slots, slots), :]
                pltpu.make_async_copy(part, part, recv_sem.at[context, expert]).wait()

    for f in range(tiles):
        for number in range(3):
            store(number, f).wait()


def backward_kernel(sizes, rows, back, place_ref, probs_ref, qh, kh, vh, gh,
                    gq_out, gk_out, gv_out, gr_out,
                    gq, gk, gv, gr, dk_sum, dv_sum, send_sem, recv_sem):
    n_expert, n_context, n_tensor = sizes
    own_expert, own_context, own_tensor = position()
    width = qh.shape[1]
    barrier = pltpu.get_barrier_semaphore()
    for step in range(1, n_context):
        pl.semaphore_signal(
            barrier, inc=1,
            device_id=(own_expert, lax.rem(own_context + step, n_context), own_tensor),
            device_id_type=MESH)
    moves = [(gr, gr_out), (gv, gv_out), (gk, gk_out), (gq, gq_out)]

    def copy(number, step):
        target = lax.rem(own_context + step, n_context)
        src, dst = moves[number]
        return remote(
            src.at[aligned(target * rows, rows), :],
            dst.at[:, aligned(own_context * width, width)],
            send_sem.at[number, step], recv_sem.at[number, step],
            (own_expert, target, own_tensor))

    def send(number):
        for step in range(1, n_context):
            copy(number, step).start()
        src, dst = moves[number]
        dst[:, aligned(own_context * width, width)] = src[aligned(own_context * rows, rows), :]

    change = dot(place_ref[...], back[0], 0, 0)
    for context in range(1, n_context):
        change = change + dot(place_ref[...], back[context], 0, 0)
    gr[...] = (gh[...].astype(jnp.float32) + change).astype(jnp.bfloat16)
    pl.semaphore_wait(barrier, n_context - 1)
    send(0)
    heads = width // HD
    dk_sum[...] = jnp.zeros_like(dk_sum)
    dv_sum[...] = jnp.zeros_like(dv_sum)
    for h in range(heads):
        cols = slice(h * HD, (h + 1) * HD)
        for c in range(n_context):
            seen = (c + 1) * rows
            block = slice(c * rows, seen)
            probs = probs_ref[h, block, :seen]
            probs32 = probs.astype(jnp.float32)
            grad_probs = dot(gr[block, cols], vh[:seen, cols], 1, 1)
            row_dot = jnp.sum(probs32 * grad_probs, axis=1, keepdims=True)
            grad_scores = (probs32 * (grad_probs - row_dot) * HD ** (-0.5)).astype(jnp.bfloat16)
            gq[block, cols] = dot(grad_scores, kh[:seen, cols]).astype(jnp.bfloat16)
            dk_sum[:seen, cols] += dot(grad_scores, qh[block, cols], 0, 0)
            dv_sum[:seen, cols] += dot(probs, gr[block, cols], 0, 0)
    gv[...] = dv_sum[...].astype(jnp.bfloat16)
    send(1)
    gk[...] = dk_sum[...].astype(jnp.bfloat16)
    send(2)
    send(3)
    for number in range(len(moves)):
        for step in range(1, n_context):
            copy(number, step).wait()


def by_heads(queries, key_input, value_input, residual, grad_output, expert_of,
             gate_weight, up_weight, down_weight):
    rows, local = queries.shape
    n_expert, n_context, n_tensor = (
        lax.axis_size("expert"), lax.axis_size("context"), lax.axis_size("tensor"))
    sizes = (n_expert, n_context, n_tensor)
    n_devices = n_expert * n_context * n_tensor
    n_all = n_expert * n_tensor
    features = local * n_tensor
    width = local // n_context
    length = rows * n_context
    hidden = gate_weight.shape[2]
    capacity = (rows // n_all + max(1, rows // (8 * n_all))) * n_context
    slots = -(-capacity // 16) * 16
    routed = n_expert * slots
    bf16, f32 = jnp.bfloat16, jnp.float32
    vmem = pl.BlockSpec(memory_space=pltpu.VMEM)
    hbm = pl.BlockSpec(memory_space=pl.ANY)
    dma = pltpu.SemaphoreType.DMA
    ids = jnp.broadcast_to(expert_of.reshape(1, rows), (n_all, rows))

    def shape(*dims):
        return jax.ShapeDtypeStruct(dims, bf16)

    x_rows, g_rows, place, probs, qh, kh, vh, gh = pl.pallas_call(
        functools.partial(forward_kernel, sizes, rows, slots),
        out_shape=[shape(routed, features), shape(routed, features),
                   shape(n_all * slots, length), shape(width // HD, length, length)]
        + [shape(length, width)] * 4,
        in_specs=[vmem] * 6,
        out_specs=[vmem] * 8,
        scratch_shapes=[
            pltpu.VMEM((length, width), bf16),
            pltpu.VMEM((n_context, n_all, rows), jnp.int32),
            pltpu.VMEM((length, width), bf16),
            pltpu.VMEM((n_all * slots, width), bf16),
            pltpu.VMEM((n_all * slots, width), bf16),
            dma((6, n_context)), dma((6, n_context)), dma((2, n_devices)), dma((2, n_devices)),
        ],
        compiler_params=pltpu.CompilerParams(
            collective_id=0, has_side_effects=True, vmem_limit_bytes=48 << 20),
    )(ids, queries, key_input, value_input, residual, grad_output)
    tile = min(hidden, 256)
    back, grad_gate, grad_up, grad_down = pl.pallas_call(
        functools.partial(expert_kernel, sizes, slots, tile),
        out_shape=[shape(n_context, n_all * slots, width), shape(*gate_weight.shape),
                   shape(*up_weight.shape), shape(*down_weight.shape)],
        in_specs=[vmem, vmem, hbm, hbm, hbm],
        out_specs=[vmem, hbm, hbm, hbm],
        scratch_shapes=[
            pltpu.VMEM((features, hidden), bf16),
            pltpu.VMEM((features, hidden), bf16),
            pltpu.VMEM((hidden, features), bf16),
            pltpu.VMEM((routed, hidden), bf16),
            pltpu.VMEM((routed, hidden), bf16),
            pltpu.VMEM((routed, hidden), bf16),
            pltpu.VMEM((routed, 1), f32),
            pltpu.VMEM((routed, 1), f32),
            pltpu.VMEM((features // width, routed, width), bf16),
            pltpu.VMEM((features, hidden), bf16),
            pltpu.VMEM((features, hidden), bf16),
            pltpu.VMEM((hidden, features), bf16),
            dma((3, hidden // tile)), dma((3, hidden // tile)),
            dma((features // width, n_expert)), dma((n_context, n_all)),
        ],
        compiler_params=pltpu.CompilerParams(
            collective_id=1, has_side_effects=True, vmem_limit_bytes=56 << 20),
    )(x_rows, g_rows, gate_weight, up_weight, down_weight)
    grad_queries, grad_keys, grad_values, grad_residual = pl.pallas_call(
        functools.partial(backward_kernel, sizes, rows),
        out_shape=[shape(rows, local)] * 4,
        in_specs=[vmem] * 7,
        out_specs=[vmem] * 4,
        scratch_shapes=[pltpu.VMEM((length, width), bf16)] * 4
        + [pltpu.VMEM((length, width), f32)] * 2
        + [dma((4, n_context)), dma((4, n_context))],
        compiler_params=pltpu.CompilerParams(
            collective_id=2, has_side_effects=True, vmem_limit_bytes=48 << 20),
    )(back, place, probs, qh, kh, vh, gh)
    return (grad_queries, grad_keys, grad_values, grad_residual, grad_gate, grad_up, grad_down)


def on_one(queries, *rest):
    if (queries.shape[1] // HD) % lax.axis_size("context") == 0:
        return by_heads(queries, *rest)
    return on_device(queries, *rest)


def solution(mesh):
    return jax.shard_map(
        on_one,
        mesh=mesh,
        in_specs=(
            P(("expert", "context"), "tensor"),
            P(("expert", "context"), "tensor"),
            P(("expert", "context"), "tensor"),
            P(("expert", "context"), "tensor"),
            P(("expert", "context"), "tensor"),
            P(("expert", "context"), None),
            P(("expert", "tensor"), None, "context"),
            P(("expert", "tensor"), None, "context"),
            P(("expert", "tensor"), "context", None),
        ),
        out_specs=(
            P(("expert", "context"), "tensor"),
            P(("expert", "context"), "tensor"),
            P(("expert", "context"), "tensor"),
            P(("expert", "context"), "tensor"),
            P(("expert", "tensor"), None, "context"),
            P(("expert", "tensor"), None, "context"),
            P(("expert", "tensor"), "context", None),
        ),
        check_vma=False,
    )
```

```python
import functools

import jax
import jax.numpy as jnp
from jax import lax
from jax.experimental import pallas as pl
from jax.experimental.pallas import tpu as pltpu
from jax.sharding import PartitionSpec as P

HD = 128
MESH = pl.DeviceIdType.MESH


EPSILON = 1e-06


def widen(array):
    return lax.optimization_barrier(array).astype(jnp.float32)


def masked_scores(query_heads, key_heads, query_start, score_scale):
    scores = (
        jnp.einsum("qhd,khd->hqk", query_heads, key_heads, preferred_element_type=jnp.float32)
        * score_scale
    )
    query_pos = query_start + jnp.arange(query_heads.shape[0], dtype=jnp.int32)
    key_pos = jnp.arange(key_heads.shape[0], dtype=jnp.int32)
    causal = key_pos[None, :] <= query_pos[:, None]
    return jnp.where(causal[None], scores, -jnp.inf)


def on_device(
    queries,
    key_input,
    value_input,
    residual,
    grad_output,
    expert_of,
    gate_weight,
    up_weight,
    down_weight,
):
    row_count = queries.shape[0]
    head_count = queries.shape[1] // HD
    n_expert = lax.axis_size("expert")
    n_tensor = lax.axis_size("tensor")
    features = queries.shape[1] * n_tensor
    score_scale = HD ** (-0.5)
    own_start = lax.axis_index("context") * row_count
    own_parity = lax.axis_index("tensor")
    all_keys, all_values = (
        lax.all_gather(key_input, "context", axis=0, tiled=True),
        lax.all_gather(value_input, "context", axis=0, tiled=True),
    )
    length = all_keys.shape[0]
    query_heads = queries.reshape(row_count, head_count, HD)
    key_heads = all_keys.reshape(length, head_count, HD)
    value_heads = all_values.reshape(length, head_count, HD)
    scores = masked_scores(query_heads, key_heads, own_start, score_scale)
    row_max = jnp.max(scores, axis=-1, keepdims=True)
    shifted = jnp.exp(scores - row_max)
    row_total = jnp.sum(shifted, axis=-1, keepdims=True)
    attn_probs = (shifted / row_total).astype(jnp.bfloat16)
    attn = jnp.einsum("hqk,khd->qhd", attn_probs, value_heads, preferred_element_type=jnp.float32)
    attn = attn.astype(jnp.bfloat16).reshape(row_count, -1)
    state = residual.astype(jnp.float32) + widen(attn)
    total_sq = lax.psum(jnp.sum(state * state, axis=-1), "tensor")
    inv_rms = (1.0 / jnp.sqrt(total_sq / features + EPSILON))[:, None]
    normed_exact = state * inv_rms
    normed = normed_exact.astype(jnp.bfloat16)
    n_all = n_expert * n_tensor
    capacity = row_count // n_all + max(1, row_count // (8 * n_all))
    expert_ids = expert_of[:, 0]
    onehot = (expert_ids[:, None] == jnp.arange(n_all, dtype=jnp.int32)[None, :]).astype(jnp.int32)
    earlier = jnp.cumsum(onehot, axis=0) - onehot
    slot_of = jnp.sum(earlier * onehot, axis=1)
    mine = expert_ids % n_tensor == own_parity
    target = jnp.where(mine, expert_ids // n_tensor * capacity + slot_of, n_expert * capacity)
    placing = (target[None, :] == jnp.arange(n_expert * capacity, dtype=jnp.int32)[:, None]).astype(
        jnp.bfloat16
    )
    full_normed, full_grad = (
        lax.all_gather(normed, "tensor", axis=1, tiled=True),
        lax.all_gather(grad_output, "tensor", axis=1, tiled=True),
    )
    send_normed = jnp.dot(placing, full_normed, preferred_element_type=jnp.float32).astype(
        jnp.bfloat16
    )
    send_grad = jnp.dot(placing, full_grad, preferred_element_type=jnp.float32).astype(jnp.bfloat16)
    send_normed = send_normed.reshape(n_expert, capacity, -1)
    send_grad = send_grad.reshape(n_expert, capacity, -1)
    got_normed, got_grad = (
        lax.all_to_all(send_normed, "expert", split_axis=0, concat_axis=0, tiled=True),
        lax.all_to_all(send_grad, "expert", split_axis=0, concat_axis=0, tiled=True),
    )
    routed_normed, routed_grad = (
        lax.all_gather(got_normed[None], "context", axis=0, tiled=True),
        lax.all_gather(got_grad[None], "context", axis=0, tiled=True),
    )
    routed_normed = routed_normed.reshape(-1, features)
    routed_grad = routed_grad.reshape(-1, features)
    gate_local = gate_weight[0]
    up_local = up_weight[0]
    down_local = down_weight[0]
    gate = jnp.dot(routed_normed, gate_local, preferred_element_type=jnp.float32)
    up_value = jnp.dot(routed_normed, up_local, preferred_element_type=jnp.float32)
    sigmoid_gate = jax.nn.sigmoid(gate)
    activation = (gate * sigmoid_gate * up_value).astype(jnp.bfloat16)
    grad_act = jnp.einsum("rd,fd->rf", routed_grad, down_local, preferred_element_type=jnp.float32)
    grad_gate_rows = (
        grad_act * up_value * sigmoid_gate * (1.0 + gate * (1.0 - sigmoid_gate))
    ).astype(jnp.bfloat16)
    grad_up_rows = (grad_act * gate * sigmoid_gate).astype(jnp.bfloat16)
    grad_down = jnp.dot(activation.T, routed_grad, preferred_element_type=jnp.float32).astype(
        jnp.bfloat16
    )[None]
    grad_gate = jnp.dot(routed_normed.T, grad_gate_rows, preferred_element_type=jnp.float32).astype(
        jnp.bfloat16
    )[None]
    grad_up = jnp.dot(routed_normed.T, grad_up_rows, preferred_element_type=jnp.float32).astype(
        jnp.bfloat16
    )[None]
    term = jnp.einsum("rf,df->rd", grad_gate_rows, gate_local, preferred_element_type=jnp.float32)
    summed_rows = lax.psum_scatter(
        term + jnp.einsum("rf,df->rd", grad_up_rows, up_local, preferred_element_type=jnp.float32),
        "context",
        scatter_dimension=0,
        tiled=True,
    )
    returned = lax.all_to_all(
        summed_rows.reshape(n_expert, capacity, -1),
        "expert",
        split_axis=0,
        concat_axis=0,
        tiled=True,
    )
    padded = jnp.concatenate(
        [returned.reshape(n_expert * capacity, -1), jnp.zeros((1, features), jnp.float32)], axis=0
    )
    full_grad_normed = jnp.take(padded, target, axis=0)
    grad_normed = lax.psum_scatter(full_grad_normed, "tensor", scatter_dimension=1, tiled=True)
    inner_sum = lax.psum(jnp.sum(normed_exact * grad_normed, axis=-1), "tensor")
    grad_state = grad_output.astype(jnp.float32) + inv_rms * (
        grad_normed - normed_exact * (inner_sum / features)[:, None]
    )
    grad_residual = grad_state.astype(jnp.bfloat16)
    grad_heads = grad_residual.reshape(row_count, head_count, HD)
    grad_probs = jnp.einsum(
        "qhd,khd->hqk", grad_heads, value_heads, preferred_element_type=jnp.float32
    )
    probs_exact = widen(attn_probs)
    row_dot = jnp.sum(probs_exact * grad_probs, axis=-1, keepdims=True)
    grad_scores = (probs_exact * (grad_probs - row_dot) * score_scale).astype(jnp.bfloat16)
    grad_queries = jnp.einsum(
        "hqk,khd->qhd", grad_scores, key_heads, preferred_element_type=jnp.float32
    )
    grad_queries = grad_queries.astype(jnp.bfloat16).reshape(row_count, -1)
    key_part = jnp.einsum(
        "hqk,qhd->khd", grad_scores, query_heads, preferred_element_type=jnp.float32
    )
    value_part = jnp.einsum(
        "hqk,qhd->khd", attn_probs, grad_heads, preferred_element_type=jnp.float32
    )
    combined = lax.psum_scatter(
        jnp.concatenate(
            [
                key_part.reshape(lax.axis_size("context") * row_count, -1),
                value_part.reshape(lax.axis_size("context") * row_count, -1),
            ],
            axis=1,
        ),
        "context",
        scatter_dimension=0,
        tiled=True,
    )
    split_at = combined.shape[1] // 2
    grad_keys = combined[:, :split_at].astype(jnp.bfloat16)
    grad_values = combined[:, split_at:].astype(jnp.bfloat16)
    return (grad_queries, grad_keys, grad_values, grad_residual, grad_gate, grad_up, grad_down)


def remote(src, dst, send_sem, recv_sem, target):
    return pltpu.make_async_remote_copy(
        src_ref=src,
        dst_ref=dst,
        send_sem=send_sem,
        recv_sem=recv_sem,
        device_id=target,
        device_id_type=MESH,
    )


def position():
    return lax.axis_index("expert"), lax.axis_index("context"), lax.axis_index("tensor")


def greet_all(sizes):
    n_expert, n_context, n_tensor = sizes
    n_devices = n_expert * n_context * n_tensor
    own_expert, own_context, own_tensor = position()
    own = (own_expert * n_context + own_context) * n_tensor + own_tensor
    barrier = pltpu.get_barrier_semaphore()

    @pl.loop(1, n_devices)
    def _(step):
        other = lax.rem(own + step, n_devices)
        target = (
            other // (n_context * n_tensor),
            lax.rem(other // n_tensor, n_context),
            lax.rem(other, n_tensor),
        )
        pl.semaphore_signal(barrier, inc=1, device_id=target, device_id_type=MESH)

    return barrier, n_devices - 1


def aligned(start, size):
    return pl.ds(pl.multiple_of(start, size), size)


def dot(left, right, left_dim=1, right_dim=0):
    return lax.dot_general(
        left, right, (((left_dim,), (right_dim,)), ((), ())), preferred_element_type=jnp.float32
    )


def as_bf16(mask):
    return mask.astype(jnp.float32).astype(jnp.bfloat16)


def layer_kernel(sizes, rows, capacity, slots, tile,
                 ids_ref, q_ref, k_ref, v_ref, r_ref, g_ref, gate_hbm, up_hbm, down_hbm,
                 gq_out, gk_out, gv_out, gr_out, down_hbm_out, x_turned, dgate, dup,
                 qh, kh, vh, rh, gh, ids_all, place_ref, probs_ref, state,
                 x_send, g_send, x_rows, g_land, g_rows,
                 gate_w, up_w, down_w, act, grad_act_ref, inv_ref, inner_ref, r_send, back,
                 down_out, gq, gk, gv, gr, dk_sum, dv_sum,
                 own_sem, in_send, in_recv, plane_send, chain_send, land_recv,
                 load_sem, store_sem, back_send, back_recv, out_send, out_recv):
    n_expert, n_context, n_tensor = sizes
    n_all = n_expert * n_tensor
    own_expert, own_context, own_tensor = position()
    own_piece = own_expert * n_tensor + own_tensor
    length, width = qh.shape
    heads = width // HD
    features, hidden = gate_w.shape
    tiles = hidden // tile
    pieces = features // width
    barrier, count = greet_all(sizes)

    def load(number, f):
        part = slice(f * tile, (f + 1) * tile)
        src, dst = ((gate_hbm.at[0, :, part], gate_w.at[:, part]),
                    (up_hbm.at[0, :, part], up_w.at[:, part]),
                    (down_hbm.at[0, part, :], down_w.at[part, :]))[number]
        return pltpu.make_async_copy(src, dst, load_sem.at[number, f])

    moves = [(q_ref, qh), (k_ref, kh), (v_ref, vh), (r_ref, rh), (g_ref, gh)]
    n_moves = len(moves)

    def own_copy(number):
        src, dst = moves[number]
        return pltpu.make_async_copy(
            src.at[:, aligned(own_context * width, width)],
            dst.at[aligned(own_context * rows, rows), :], own_sem.at[number])

    for number in range(n_moves):
        own_copy(number).start()
    ids_all[own_context] = ids_ref[...]

    def in_copy(number, step):
        target = lax.rem(own_context + step, n_context)
        if number == n_moves:
            src, dst = ids_ref, ids_all.at[own_context]
        else:
            src = moves[number][0].at[:, aligned(target * width, width)]
            dst = moves[number][1].at[aligned(own_context * rows, rows), :]
        return remote(src, dst, in_send.at[number, step], in_recv.at[number, step],
                      (own_expert, target, own_tensor))

    def start_in(number):
        for step in range(1, n_context):
            in_copy(number, step).start()

    def arrived(number):
        for step in range(1, n_context):
            in_copy(number, step).wait_recv()
        if number < n_moves:
            own_copy(number).wait()

    def land(kind, plane, piece):
        if kind == 0:
            return g_land.at[piece, plane]
        seq, tensor = piece // n_tensor, lax.rem(piece, n_tensor)
        return x_rows.at[aligned(seq * slots, slots),
                         aligned((tensor * n_context + plane) * width, width)]

    def plane_copy(kind, step):
        other = lax.rem(own_piece + step, n_all)
        src = (g_send, x_send)[kind]
        return remote(
            src.at[aligned(other * slots, slots), :], land(kind, own_context, own_piece),
            plane_send.at[kind, step], land_recv.at[kind, own_context, own_piece],
            (other // n_tensor, own_context, lax.rem(other, n_tensor)))

    def chain_copy(kind, plane, piece, side):
        part = land(kind, plane, piece)
        return remote(
            part, part, chain_send.at[kind, side, plane, piece], land_recv.at[kind, plane, piece],
            (own_expert, own_context + (1, -1)[side], own_tensor))

    def await_land(kind, plane, piece):
        part = land(kind, plane, piece)
        pltpu.make_async_copy(part, part, land_recv.at[kind, plane, piece]).wait()

    has = (own_context < n_context - 1, own_context > 0)

    def start_plane(kind):
        @pl.loop(1, n_all)
        def _(step):
            plane_copy(kind, step).start()

        src = (g_send, x_send)[kind]
        mine = src[aligned(own_piece * slots, slots), :]
        if kind == 0:
            g_land[own_piece, own_context] = mine
        else:
            x_rows[aligned(own_expert * slots, slots),
                   aligned((own_tensor * n_context + own_context) * width, width)] = mine

    def pass_on(kind, away):
        if away == 0:
            @pl.loop(0, n_all)
            def _(turn):
                piece = lax.rem(own_piece + turn, n_all)

                @pl.when(piece != own_piece)
                def _():
                    await_land(kind, own_context, piece)

                for side in (0, 1):
                    @pl.when(has[side])
                    def _():
                        chain_copy(kind, own_context, piece, side).start()
            return
        for side in (0, 1):
            plane = own_context + (-away, away)[side]

            @pl.when((plane >= 0) & (plane < n_context))
            def _():
                @pl.loop(0, n_all)
                def _(piece):
                    await_land(kind, plane, piece)

                    @pl.when(has[side])
                    def _():
                        chain_copy(kind, plane, piece, side).start()

    def chain_sent(kind):
        @pl.loop(1, n_all)
        def _(step):
            plane_copy(kind, step).wait_send()

        for away in range(n_context - 1):
            for side in (0, 1):
                plane = own_context + (-away, away)[side]

                @pl.when((plane >= 0) & (plane < n_context) & has[side])
                def _():
                    @pl.loop(0, n_all)
                    def _(piece):
                        chain_copy(kind, plane, piece, side).wait_send()

    named = lax.broadcasted_iota(jnp.int32, (n_all, rows), 0)
    before = as_bf16(lax.broadcasted_iota(jnp.int32, (rows, rows), 0)
                     < lax.broadcasted_iota(jnp.int32, (rows, rows), 1))
    slot = lax.broadcasted_iota(jnp.int32, (slots, rows), 0).astype(jnp.float32)

    def ranks(ids):
        onehot = (ids == named).astype(jnp.float32)
        return jnp.where(onehot > 0.5, dot(onehot.astype(jnp.bfloat16), before), -2.0 * slots)

    own_rank = ranks(ids_ref[...])
    pl.semaphore_wait(barrier, count)
    for number in (n_moves, 0, 1, 2, 3):
        start_in(number)
    for f in range(tiles):
        for number in (2, 0, 1):
            load(number, f).start()
    for e in range(n_all):
        packed = jnp.zeros((slots, width), jnp.float32)
        for j in range(n_context):
            place = as_bf16(own_rank[e:e + 1, :] + j * capacity == slot)
            packed = packed + dot(place, g_ref[:, j * width:(j + 1) * width])
        g_send[e * slots:(e + 1) * slots, :] = packed.astype(jnp.bfloat16)
    start_plane(0)
    arrived(n_moves)
    for c in range(n_context):
        rank = ranks(ids_all[c])
        for e in range(n_all):
            place_ref[e * slots:(e + 1) * slots, c * rows:(c + 1) * rows] = as_bf16(
                rank[e:e + 1, :] + c * capacity == slot)
    pass_on(0, 0)
    for number in range(4):
        arrived(number)
    for h in range(heads):
        cols = slice(h * HD, (h + 1) * HD)
        for c in range(n_context):
            seen = (c + 1) * rows
            block = slice(c * rows, seen)
            scores = dot(qh[block, cols], kh[:seen, cols], 1, 1) * HD ** (-0.5)
            query = c * rows + lax.broadcasted_iota(jnp.int32, (rows, seen), 0)
            key = lax.broadcasted_iota(jnp.int32, (rows, seen), 1)
            scores = jnp.where(key <= query, scores, -jnp.inf)
            shifted = jnp.exp(scores - jnp.max(scores, axis=1, keepdims=True))
            probs = (shifted / jnp.sum(shifted, axis=1, keepdims=True)).astype(jnp.bfloat16)
            probs_ref[h, block, :seen] = probs
            attn = dot(probs, vh[:seen, cols]).astype(jnp.bfloat16).astype(jnp.float32)
            state[block, cols] = (rh[block, cols].astype(jnp.float32) + attn).astype(jnp.bfloat16)
        if h == 0:
            pass_on(0, 1)
    for e in range(n_all):
        x_send[e * slots:(e + 1) * slots, :] = dot(
            place_ref[e * slots:(e + 1) * slots, :], state[...]).astype(jnp.bfloat16)
    start_plane(1)
    for away in range(2, n_context):
        pass_on(0, away)
        if away == 2:
            pass_on(1, 0)
    if n_context == 2:
        pass_on(1, 0)
    pass_on(1, 1)

    out_row = lax.broadcasted_iota(jnp.int32, (slots, n_context * slots), 0)
    in_row = lax.broadcasted_iota(jnp.int32, (slots, n_context * slots), 1)
    unpack = []
    for j in range(n_context):
        match = jnp.zeros((slots, n_context * slots), jnp.float32)
        for c in range(n_context):
            match = match + (
                (in_row == out_row + c * (slots - capacity) + j * capacity)
                & (out_row >= c * capacity) & (out_row < (c + 1) * capacity)).astype(jnp.float32)
        unpack.append(match)
    unpack = jnp.concatenate(unpack, axis=0).astype(jnp.bfloat16)
    for seq in range(n_expert):
        for t in range(n_tensor):
            landed = g_land[seq * n_tensor + t].reshape(n_context * slots, width)
            parts = dot(unpack, landed).astype(jnp.bfloat16)
            for j in range(n_context):
                at = (t * n_context + j) * width
                g_rows[seq * slots:(seq + 1) * slots, at:at + width] = parts[
                    j * slots:(j + 1) * slots]
    for away in range(2, n_context):
        pass_on(1, away)
        if away == 2:
            start_in(4)
    if n_context == 2:
        start_in(4)
    for f in range(tiles):
        part = slice(f * tile, (f + 1) * tile)
        for number in range(3):
            load(number, f).wait()
        grad_act_ref[:, part] = dot(g_rows[...], down_w[part, :], 1, 1)

    x32 = x_rows[...].astype(jnp.float32)
    inv_ref[...] = 1.0 / jnp.sqrt(
        jnp.sum(x32 * x32, axis=1, keepdims=True) / features + EPSILON)
    inner_ref[...] = jnp.zeros_like(inner_ref)
    for f in range(tiles):
        part = slice(f * tile, (f + 1) * tile)
        inv = inv_ref[...]
        gate = dot(x_rows[...], gate_w[:, part]) * inv
        up = dot(x_rows[...], up_w[:, part]) * inv
        grad_act = grad_act_ref[:, part]
        sig = 1.0 / (1.0 + jnp.exp(-gate))
        grad_up = grad_act * gate * sig
        grad_gate = grad_act * up * sig * (1.0 + gate * (1.0 - sig))
        act[:, part] = (gate * sig * up).astype(jnp.bfloat16)
        inner_ref[...] += jnp.sum(grad_gate * gate + grad_up * up, axis=1, keepdims=True)
        dgate[:, part] = (grad_gate * inv).astype(jnp.bfloat16)
        dup[:, part] = (grad_up * inv).astype(jnp.bfloat16)
    inner_ref[...] = inner_ref[...] * inv_ref[...] * inv_ref[...] / features

    def piece_copy(piece, seq):
        tensor, context = piece // n_context, lax.rem(piece, n_context)
        return remote(
            r_send.at[piece, aligned(seq * slots, slots), :],
            back.at[own_context, aligned(own_piece * slots, slots), :],
            back_send.at[piece, seq], back_recv.at[own_context, own_piece],
            (seq, context, tensor))

    def is_own(piece, seq):
        return (piece == own_tensor * n_context + own_context) & (seq == own_expert)

    @pl.loop(0, pieces)
    def _(turn):
        piece = lax.rem(own_tensor * n_context + own_context + 1 + turn, pieces)
        part = aligned(piece * width, width)
        grad = dot(dgate[...], gate_w[part, :], 1, 1) + dot(dup[...], up_w[part, :], 1, 1)
        grad = grad - x_rows[:, part].astype(jnp.float32) * inner_ref[...]
        r_send[piece] = grad.astype(jnp.bfloat16)

        @pl.loop(0, n_expert)
        def _(seq):
            @pl.when(jnp.logical_not(is_own(piece, seq)))
            def _():
                piece_copy(piece, seq).start()

    back[own_context, aligned(own_piece * slots, slots), :] = r_send[
        own_tensor * n_context + own_context, aligned(own_expert * slots, slots), :]

    def store(f):
        part = slice(f * tile, (f + 1) * tile)
        return pltpu.make_async_copy(
            down_out.at[part, :], down_hbm_out.at[0, part, :], store_sem.at[f])

    for f in range(tiles):
        part = slice(f * tile, (f + 1) * tile)
        down_out[part, :] = dot(act[:, part], g_rows[...], 0, 0).astype(jnp.bfloat16)
        store(f).start()
    x_turned[...] = x_rows[...].T
    chain_sent(0)
    chain_sent(1)
    arrived(4)
    for number in range(n_moves + 1):
        for step in range(1, n_context):
            in_copy(number, step).wait_send()

    @pl.loop(0, n_context)
    def _(context):
        @pl.loop(0, n_all)
        def _(piece):
            @pl.when(jnp.logical_not((context == own_context) & (piece == own_piece)))
            def _():
                part = back.at[context, aligned(piece * slots, slots), :]
                pltpu.make_async_copy(part, part, back_recv.at[context, piece]).wait()

    outs = [(gr, gr_out), (gv, gv_out), (gk, gk_out), (gq, gq_out)]

    def out_copy(number, step):
        target = lax.rem(own_context + step, n_context)
        src, dst = outs[number]
        return remote(
            src.at[aligned(target * rows, rows), :],
            dst.at[:, aligned(own_context * width, width)],
            out_send.at[number, step], out_recv.at[number, step],
            (own_expert, target, own_tensor))

    def send(number):
        for step in range(1, n_context):
            out_copy(number, step).start()
        src, dst = outs[number]
        dst[:, aligned(own_context * width, width)] = src[aligned(own_context * rows, rows), :]

    change = dot(place_ref[...], back[0], 0, 0)
    for context in range(1, n_context):
        change = change + dot(place_ref[...], back[context], 0, 0)
    gr[...] = (gh[...].astype(jnp.float32) + change).astype(jnp.bfloat16)
    send(0)
    dk_sum[...] = jnp.zeros_like(dk_sum)
    dv_sum[...] = jnp.zeros_like(dv_sum)
    for h in range(heads):
        cols = slice(h * HD, (h + 1) * HD)
        for c in range(n_context):
            seen = (c + 1) * rows
            block = slice(c * rows, seen)
            dv_sum[:seen, cols] += dot(probs_ref[h, block, :seen], gr[block, cols], 0, 0)
    gv[...] = dv_sum[...].astype(jnp.bfloat16)
    send(1)
    for h in range(heads):
        cols = slice(h * HD, (h + 1) * HD)
        for c in range(n_context):
            seen = (c + 1) * rows
            block = slice(c * rows, seen)
            probs = probs_ref[h, block, :seen].astype(jnp.float32)
            grad_probs = dot(gr[block, cols], vh[:seen, cols], 1, 1)
            row_dot = jnp.sum(probs * grad_probs, axis=1, keepdims=True)
            grad_scores = (probs * (grad_probs - row_dot) * HD ** (-0.5)).astype(jnp.bfloat16)
            gq[block, cols] = dot(grad_scores, kh[:seen, cols]).astype(jnp.bfloat16)
            dk_sum[:seen, cols] += dot(grad_scores, qh[block, cols], 0, 0)
    gk[...] = dk_sum[...].astype(jnp.bfloat16)
    send(2)
    send(3)

    @pl.loop(0, pieces)
    def _(piece):
        @pl.loop(0, n_expert)
        def _(seq):
            @pl.when(jnp.logical_not(is_own(piece, seq)))
            def _():
                piece_copy(piece, seq).wait_send()

    for f in range(tiles):
        store(f).wait()
    for number in range(len(outs)):
        for step in range(1, n_context):
            out_copy(number, step).wait()


def finish_kernel(tile, x_turned, dgate, dup, *refs):
    given, written = refs[:5], refs[5:10]
    grad_gate_hbm, grad_up_hbm, gate_out, up_out, copy_sem, store_sem = refs[10:]
    copies = [pltpu.make_async_copy(src, dst, copy_sem.at[i])
              for i, (src, dst) in enumerate(zip(given, written))]
    for copy in copies:
        copy.start()
    stores = []
    for f in range(dgate.shape[1] // tile):
        part = slice(f * tile, (f + 1) * tile)
        for number, (rows_ref, out, hbm) in enumerate(
                ((dgate, gate_out, grad_gate_hbm), (dup, up_out, grad_up_hbm))):
            out[:, part] = dot(x_turned[...], rows_ref[:, part]).astype(jnp.bfloat16)
            stores.append(pltpu.make_async_copy(
                out.at[:, part], hbm.at[0, :, part], store_sem.at[number, f]))
            stores[-1].start()
    for copy in copies + stores:
        copy.wait()


def by_heads(queries, key_input, value_input, residual, grad_output, expert_of,
             gate_weight, up_weight, down_weight):
    rows, local = queries.shape
    n_expert, n_context, n_tensor = (
        lax.axis_size("expert"), lax.axis_size("context"), lax.axis_size("tensor"))
    sizes = (n_expert, n_context, n_tensor)
    n_all = n_expert * n_tensor
    features = local * n_tensor
    width = local // n_context
    length = rows * n_context
    hidden = gate_weight.shape[2]
    capacity = rows // n_all + max(1, rows // (8 * n_all))
    slots = -(-capacity * n_context // 16) * 16
    routed = n_expert * slots
    tile = min(hidden, 256)
    tiles = hidden // tile
    bf16, f32 = jnp.bfloat16, jnp.float32
    vmem = pl.BlockSpec(memory_space=pltpu.VMEM)
    hbm = pl.BlockSpec(memory_space=pl.ANY)
    dma = pltpu.SemaphoreType.DMA
    ids = jnp.broadcast_to(expert_of.reshape(1, rows), (n_all, rows))

    def shape(*dims):
        return jax.ShapeDtypeStruct(dims, bf16)

    def scratch(*dims, dtype=bf16):
        return pltpu.VMEM(dims, dtype)

    by_head = scratch(length, width)
    *small, down_grad, x_turned, dgate, dup = pl.pallas_call(
        functools.partial(layer_kernel, sizes, rows, capacity, slots, tile),
        out_shape=[shape(rows, local)] * 4
        + [shape(*down_weight.shape), shape(features, routed),
           shape(routed, hidden), shape(routed, hidden)],
        in_specs=[vmem, hbm, hbm, hbm, hbm, vmem, hbm, hbm, hbm],
        out_specs=[vmem] * 4 + [hbm] + [vmem] * 3,
        scratch_shapes=[
            by_head, by_head, by_head, by_head, by_head,
            scratch(n_context, n_all, rows, dtype=jnp.int32),
            scratch(n_all * slots, length),
            scratch(width // HD, length, length),
            by_head,
            scratch(n_all * slots, width),
            scratch(n_all * slots, width),
            scratch(routed, features),
            scratch(n_all, n_context, slots, width),
            scratch(routed, features),
            scratch(features, hidden),
            scratch(features, hidden),
            scratch(hidden, features),
            scratch(routed, hidden),
            scratch(routed, hidden, dtype=f32),
            scratch(routed, 1, dtype=f32),
            scratch(routed, 1, dtype=f32),
            scratch(features // width, routed, width),
            scratch(n_context, n_all * slots, width),
            scratch(hidden, features),
            by_head, by_head, by_head, by_head,
            scratch(length, width, dtype=f32),
            scratch(length, width, dtype=f32),
            dma((5,)), dma((6, n_context)), dma((6, n_context)),
            dma((2, n_all)), dma((2, 2, n_context, n_all)), dma((2, n_context, n_all)),
            dma((3, tiles)), dma((tiles,)),
            dma((features // width, n_expert)), dma((n_context, n_all)),
            dma((4, n_context)), dma((4, n_context)),
        ],
        compiler_params=pltpu.CompilerParams(
            collective_id=0, has_side_effects=True, vmem_limit_bytes=52 << 20),
    )(ids, queries, key_input, value_input, residual, grad_output,
      gate_weight, up_weight, down_weight)
    *small, down_grad, gate_grad, up_grad = pl.pallas_call(
        functools.partial(finish_kernel, tile),
        out_shape=[shape(rows, local)] * 4
        + [shape(*down_weight.shape), shape(*gate_weight.shape), shape(*up_weight.shape)],
        in_specs=[vmem] * 3 + [hbm] * 5,
        out_specs=[hbm] * 7,
        scratch_shapes=[
            scratch(features, hidden), scratch(features, hidden), dma((5,)), dma((2, tiles))],
        compiler_params=pltpu.CompilerParams(vmem_limit_bytes=24 << 20),
    )(x_turned, dgate, dup, *small, down_grad)
    return (*small, gate_grad, up_grad, down_grad)


def on_one(queries, *rest):
    if (queries.shape[1] // HD) % lax.axis_size("context") == 0:
        return by_heads(queries, *rest)
    return on_device(queries, *rest)


def solution(mesh):
    return jax.shard_map(
        on_one,
        mesh=mesh,
        in_specs=(
            P(("expert", "context"), "tensor"),
            P(("expert", "context"), "tensor"),
            P(("expert", "context"), "tensor"),
            P(("expert", "context"), "tensor"),
            P(("expert", "context"), "tensor"),
            P(("expert", "context"), None),
            P(("expert", "tensor"), None, "context"),
            P(("expert", "tensor"), None, "context"),
            P(("expert", "tensor"), "context", None),
        ),
        out_specs=(
            P(("expert", "context"), "tensor"),
            P(("expert", "context"), "tensor"),
            P(("expert", "context"), "tensor"),
            P(("expert", "context"), "tensor"),
            P(("expert", "tensor"), None, "context"),
            P(("expert", "tensor"), None, "context"),
            P(("expert", "tensor"), "context", None),
        ),
        check_vma=False,
    )
```

```python
import functools

import jax
import jax.numpy as jnp
from jax import lax
from jax.experimental import pallas as pl
from jax.experimental.pallas import tpu as pltpu
from jax.sharding import PartitionSpec as P

HD = 128
MESH = pl.DeviceIdType.MESH


EPSILON = 1e-06


def widen(array):
    return lax.optimization_barrier(array).astype(jnp.float32)


def masked_scores(query_heads, key_heads, query_start, score_scale):
    scores = (
        jnp.einsum("qhd,khd->hqk", query_heads, key_heads, preferred_element_type=jnp.float32)
        * score_scale
    )
    query_pos = query_start + jnp.arange(query_heads.shape[0], dtype=jnp.int32)
    key_pos = jnp.arange(key_heads.shape[0], dtype=jnp.int32)
    causal = key_pos[None, :] <= query_pos[:, None]
    return jnp.where(causal[None], scores, -jnp.inf)


def on_device(
    queries,
    key_input,
    value_input,
    residual,
    grad_output,
    expert_of,
    gate_weight,
    up_weight,
    down_weight,
):
    row_count = queries.shape[0]
    head_count = queries.shape[1] // HD
    n_expert = lax.axis_size("expert")
    n_tensor = lax.axis_size("tensor")
    features = queries.shape[1] * n_tensor
    score_scale = HD ** (-0.5)
    own_start = lax.axis_index("context") * row_count
    own_parity = lax.axis_index("tensor")
    all_keys, all_values = (
        lax.all_gather(key_input, "context", axis=0, tiled=True),
        lax.all_gather(value_input, "context", axis=0, tiled=True),
    )
    length = all_keys.shape[0]
    query_heads = queries.reshape(row_count, head_count, HD)
    key_heads = all_keys.reshape(length, head_count, HD)
    value_heads = all_values.reshape(length, head_count, HD)
    scores = masked_scores(query_heads, key_heads, own_start, score_scale)
    row_max = jnp.max(scores, axis=-1, keepdims=True)
    shifted = jnp.exp(scores - row_max)
    row_total = jnp.sum(shifted, axis=-1, keepdims=True)
    attn_probs = (shifted / row_total).astype(jnp.bfloat16)
    attn = jnp.einsum("hqk,khd->qhd", attn_probs, value_heads, preferred_element_type=jnp.float32)
    attn = attn.astype(jnp.bfloat16).reshape(row_count, -1)
    state = residual.astype(jnp.float32) + widen(attn)
    total_sq = lax.psum(jnp.sum(state * state, axis=-1), "tensor")
    inv_rms = (1.0 / jnp.sqrt(total_sq / features + EPSILON))[:, None]
    normed_exact = state * inv_rms
    normed = normed_exact.astype(jnp.bfloat16)
    n_all = n_expert * n_tensor
    capacity = row_count // n_all + max(1, row_count // (8 * n_all))
    expert_ids = expert_of[:, 0]
    onehot = (expert_ids[:, None] == jnp.arange(n_all, dtype=jnp.int32)[None, :]).astype(jnp.int32)
    earlier = jnp.cumsum(onehot, axis=0) - onehot
    slot_of = jnp.sum(earlier * onehot, axis=1)
    mine = expert_ids % n_tensor == own_parity
    target = jnp.where(mine, expert_ids // n_tensor * capacity + slot_of, n_expert * capacity)
    placing = (target[None, :] == jnp.arange(n_expert * capacity, dtype=jnp.int32)[:, None]).astype(
        jnp.bfloat16
    )
    full_normed, full_grad = (
        lax.all_gather(normed, "tensor", axis=1, tiled=True),
        lax.all_gather(grad_output, "tensor", axis=1, tiled=True),
    )
    send_normed = jnp.dot(placing, full_normed, preferred_element_type=jnp.float32).astype(
        jnp.bfloat16
    )
    send_grad = jnp.dot(placing, full_grad, preferred_element_type=jnp.float32).astype(jnp.bfloat16)
    send_normed = send_normed.reshape(n_expert, capacity, -1)
    send_grad = send_grad.reshape(n_expert, capacity, -1)
    got_normed, got_grad = (
        lax.all_to_all(send_normed, "expert", split_axis=0, concat_axis=0, tiled=True),
        lax.all_to_all(send_grad, "expert", split_axis=0, concat_axis=0, tiled=True),
    )
    routed_normed, routed_grad = (
        lax.all_gather(got_normed[None], "context", axis=0, tiled=True),
        lax.all_gather(got_grad[None], "context", axis=0, tiled=True),
    )
    routed_normed = routed_normed.reshape(-1, features)
    routed_grad = routed_grad.reshape(-1, features)
    gate_local = gate_weight[0]
    up_local = up_weight[0]
    down_local = down_weight[0]
    gate = jnp.dot(routed_normed, gate_local, preferred_element_type=jnp.float32)
    up_value = jnp.dot(routed_normed, up_local, preferred_element_type=jnp.float32)
    sigmoid_gate = jax.nn.sigmoid(gate)
    activation = (gate * sigmoid_gate * up_value).astype(jnp.bfloat16)
    grad_act = jnp.einsum("rd,fd->rf", routed_grad, down_local, preferred_element_type=jnp.float32)
    grad_gate_rows = (
        grad_act * up_value * sigmoid_gate * (1.0 + gate * (1.0 - sigmoid_gate))
    ).astype(jnp.bfloat16)
    grad_up_rows = (grad_act * gate * sigmoid_gate).astype(jnp.bfloat16)
    grad_down = jnp.dot(activation.T, routed_grad, preferred_element_type=jnp.float32).astype(
        jnp.bfloat16
    )[None]
    grad_gate = jnp.dot(routed_normed.T, grad_gate_rows, preferred_element_type=jnp.float32).astype(
        jnp.bfloat16
    )[None]
    grad_up = jnp.dot(routed_normed.T, grad_up_rows, preferred_element_type=jnp.float32).astype(
        jnp.bfloat16
    )[None]
    term = jnp.einsum("rf,df->rd", grad_gate_rows, gate_local, preferred_element_type=jnp.float32)
    summed_rows = lax.psum_scatter(
        term + jnp.einsum("rf,df->rd", grad_up_rows, up_local, preferred_element_type=jnp.float32),
        "context",
        scatter_dimension=0,
        tiled=True,
    )
    returned = lax.all_to_all(
        summed_rows.reshape(n_expert, capacity, -1),
        "expert",
        split_axis=0,
        concat_axis=0,
        tiled=True,
    )
    padded = jnp.concatenate(
        [returned.reshape(n_expert * capacity, -1), jnp.zeros((1, features), jnp.float32)], axis=0
    )
    full_grad_normed = jnp.take(padded, target, axis=0)
    grad_normed = lax.psum_scatter(full_grad_normed, "tensor", scatter_dimension=1, tiled=True)
    inner_sum = lax.psum(jnp.sum(normed_exact * grad_normed, axis=-1), "tensor")
    grad_state = grad_output.astype(jnp.float32) + inv_rms * (
        grad_normed - normed_exact * (inner_sum / features)[:, None]
    )
    grad_residual = grad_state.astype(jnp.bfloat16)
    grad_heads = grad_residual.reshape(row_count, head_count, HD)
    grad_probs = jnp.einsum(
        "qhd,khd->hqk", grad_heads, value_heads, preferred_element_type=jnp.float32
    )
    probs_exact = widen(attn_probs)
    row_dot = jnp.sum(probs_exact * grad_probs, axis=-1, keepdims=True)
    grad_scores = (probs_exact * (grad_probs - row_dot) * score_scale).astype(jnp.bfloat16)
    grad_queries = jnp.einsum(
        "hqk,khd->qhd", grad_scores, key_heads, preferred_element_type=jnp.float32
    )
    grad_queries = grad_queries.astype(jnp.bfloat16).reshape(row_count, -1)
    key_part = jnp.einsum(
        "hqk,qhd->khd", grad_scores, query_heads, preferred_element_type=jnp.float32
    )
    value_part = jnp.einsum(
        "hqk,qhd->khd", attn_probs, grad_heads, preferred_element_type=jnp.float32
    )
    combined = lax.psum_scatter(
        jnp.concatenate(
            [
                key_part.reshape(lax.axis_size("context") * row_count, -1),
                value_part.reshape(lax.axis_size("context") * row_count, -1),
            ],
            axis=1,
        ),
        "context",
        scatter_dimension=0,
        tiled=True,
    )
    split_at = combined.shape[1] // 2
    grad_keys = combined[:, :split_at].astype(jnp.bfloat16)
    grad_values = combined[:, split_at:].astype(jnp.bfloat16)
    return (grad_queries, grad_keys, grad_values, grad_residual, grad_gate, grad_up, grad_down)


LANES = 128


def remote(src, dst, send_sem, recv_sem, target):
    return pltpu.make_async_remote_copy(
        src_ref=src,
        dst_ref=dst,
        send_sem=send_sem,
        recv_sem=recv_sem,
        device_id=target,
        device_id_type=MESH,
    )


def position():
    return lax.axis_index("expert"), lax.axis_index("context"), lax.axis_index("tensor")


def greet_all(sizes):
    n_expert, n_context, n_tensor = sizes
    n_devices = n_expert * n_context * n_tensor
    own_expert, own_context, own_tensor = position()
    own = (own_expert * n_context + own_context) * n_tensor + own_tensor
    barrier = pltpu.get_barrier_semaphore()

    @pl.loop(1, n_devices)
    def _(step):
        other = lax.rem(own + step, n_devices)
        target = (
            other // (n_context * n_tensor),
            lax.rem(other // n_tensor, n_context),
            lax.rem(other, n_tensor),
        )
        pl.semaphore_signal(barrier, inc=1, device_id=target, device_id_type=MESH)

    return barrier, n_devices - 1


def aligned(start, size):
    return pl.ds(pl.multiple_of(start, size), size)


def dot(left, right, left_dim=1, right_dim=0):
    return lax.dot_general(
        left, right, (((left_dim,), (right_dim,)), ((), ())), preferred_element_type=jnp.float32
    )


def as_bf16(mask):
    return mask.astype(jnp.float32).astype(jnp.bfloat16)


def pack(ref, at, value, rows):
    for b in range(value.shape[1] // LANES):
        ref[(*at, slice(b * rows, (b + 1) * rows), slice(None))] = value[
            :, b * LANES:(b + 1) * LANES]


def unpacked(ref, at, rows, width):
    return jnp.concatenate(
        [ref[(*at, slice(b * rows, (b + 1) * rows), slice(None))]
         for b in range(width // LANES)], axis=1)


def layer_kernel(sizes, rows, capacity, slots, tile,
                 ids_ref, q_ref, k_ref, v_ref, r_ref, g_ref, gate_hbm, up_hbm, down_hbm,
                 gq_out, gk_out, gv_out, gr_out, down_hbm_out, x_turned, dgate, dup,
                 qh, kh, vh, rh, gh, ids_all, place_ref, probs_ref, state,
                 x_send, g_send, x_land, g_land, x_rows, g_rows,
                 gate_w, up_w, down_w, act, grad_act_ref, inv_ref, inner_ref, r_send, back, pair_land,
                 down_out, gq, gk, gv, gr, dk_sum, dv_sum,
                 own_sem, in_send, in_recv, plane_send, chain_send, land_recv,
                 load_sem, store_sem, back_send, back_recv, pair_send, pair_recv, out_send, out_recv):
    n_expert, n_context, n_tensor = sizes
    n_all = n_expert * n_tensor
    own_expert, own_context, own_tensor = position()
    own_piece = own_expert * n_tensor + own_tensor
    length, width = qh.shape
    heads = width // HD
    features, hidden = gate_w.shape
    tiles = hidden // tile
    pieces = features // width
    barrier, count = greet_all(sizes)

    def load(number, f):
        part = slice(f * tile, (f + 1) * tile)
        src, dst = ((gate_hbm.at[0, :, part], gate_w.at[:, part]),
                    (up_hbm.at[0, :, part], up_w.at[:, part]),
                    (down_hbm.at[0, part, :], down_w.at[part, :]))[number]
        return pltpu.make_async_copy(src, dst, load_sem.at[number, f])

    moves = [(q_ref, qh), (k_ref, kh), (v_ref, vh), (r_ref, rh), (g_ref, gh)]
    n_moves = len(moves)

    def own_copy(number):
        src, dst = moves[number]
        return pltpu.make_async_copy(
            src.at[:, aligned(own_context * width, width)],
            dst.at[aligned(own_context * rows, rows), :], own_sem.at[number])

    for number in range(n_moves):
        own_copy(number).start()
    ids_all[own_context] = ids_ref[...]

    def in_copy(number, step):
        target = lax.rem(own_context + step, n_context)
        if number == n_moves:
            src, dst = ids_ref, ids_all.at[own_context]
        else:
            src = moves[number][0].at[:, aligned(target * width, width)]
            dst = moves[number][1].at[aligned(own_context * rows, rows), :]
        return remote(src, dst, in_send.at[number, step], in_recv.at[number, step],
                      (own_expert, target, own_tensor))

    def start_in(number):
        for step in range(1, n_context):
            in_copy(number, step).start()

    def arrived(number):
        for step in range(1, n_context):
            in_copy(number, step).wait_recv()
        if number < n_moves:
            own_copy(number).wait()

    def land(kind, plane, piece):
        return (g_land, x_land)[kind].at[piece, plane]

    def plane_copy(kind, step):
        other = lax.rem(own_piece + step, n_all)
        src = (g_send, x_send)[kind]
        return remote(
            src.at[other], land(kind, own_context, own_piece),
            plane_send.at[kind, step], land_recv.at[kind, own_context, own_piece],
            (other // n_tensor, own_context, lax.rem(other, n_tensor)))

    def chain_copy(kind, plane, piece, side):
        part = land(kind, plane, piece)
        return remote(
            part, part, chain_send.at[kind, side, plane, piece], land_recv.at[kind, plane, piece],
            (own_expert, own_context + (1, -1)[side], own_tensor))

    def await_land(kind, plane, piece):
        part = land(kind, plane, piece)
        pltpu.make_async_copy(part, part, land_recv.at[kind, plane, piece]).wait()

    has = (own_context < n_context - 1, own_context > 0)

    def start_plane(kind):
        @pl.loop(1, n_all)
        def _(step):
            plane_copy(kind, step).start()

        (g_land, x_land)[kind][own_piece, own_context] = (g_send, x_send)[kind][own_piece]

    def pass_on(kind, away):
        if away == 0:
            @pl.loop(0, n_all)
            def _(turn):
                piece = lax.rem(own_piece + turn, n_all)

                @pl.when(piece != own_piece)
                def _():
                    await_land(kind, own_context, piece)

                for side in (0, 1):
                    @pl.when(has[side])
                    def _():
                        chain_copy(kind, own_context, piece, side).start()
            return
        for side in (0, 1):
            plane = own_context + (-away, away)[side]

            @pl.when((plane >= 0) & (plane < n_context))
            def _():
                @pl.loop(0, n_all)
                def _(piece):
                    await_land(kind, plane, piece)

                    @pl.when(has[side])
                    def _():
                        chain_copy(kind, plane, piece, side).start()

    def chain_sent(kind):
        @pl.loop(1, n_all)
        def _(step):
            plane_copy(kind, step).wait_send()

        for away in range(n_context - 1):
            for side in (0, 1):
                plane = own_context + (-away, away)[side]

                @pl.when((plane >= 0) & (plane < n_context) & has[side])
                def _():
                    @pl.loop(0, n_all)
                    def _(piece):
                        chain_copy(kind, plane, piece, side).wait_send()

    named = lax.broadcasted_iota(jnp.int32, (n_all, rows), 0)
    before = as_bf16(lax.broadcasted_iota(jnp.int32, (rows, rows), 0)
                     < lax.broadcasted_iota(jnp.int32, (rows, rows), 1))
    slot = lax.broadcasted_iota(jnp.int32, (slots, rows), 0).astype(jnp.float32)

    def ranks(ids):
        onehot = (ids == named).astype(jnp.float32)
        return jnp.where(onehot > 0.5, dot(onehot.astype(jnp.bfloat16), before), -2.0 * slots)

    own_rank = ranks(ids_ref[...])
    pl.semaphore_wait(barrier, count)
    for number in (n_moves, 0, 1, 2, 3):
        start_in(number)
    for f in range(tiles):
        for number in (2, 0, 1):
            load(number, f).start()
    for e in range(n_all):
        packed = jnp.zeros((slots, width), jnp.float32)
        for j in range(n_context):
            place = as_bf16(own_rank[e:e + 1, :] + j * capacity == slot)
            packed = packed + dot(place, g_ref[:, j * width:(j + 1) * width])
        pack(g_send, (e,), packed.astype(jnp.bfloat16), slots)
    start_plane(0)
    arrived(n_moves)
    for c in range(n_context):
        rank = ranks(ids_all[c])
        for e in range(n_all):
            place_ref[e * slots:(e + 1) * slots, c * rows:(c + 1) * rows] = as_bf16(
                rank[e:e + 1, :] + c * capacity == slot)
    pass_on(0, 0)
    for number in range(4):
        arrived(number)
    for h in range(heads):
        cols = slice(h * HD, (h + 1) * HD)
        for c in range(n_context):
            seen = (c + 1) * rows
            block = slice(c * rows, seen)
            scores = dot(qh[block, cols], kh[:seen, cols], 1, 1) * HD ** (-0.5)
            query = c * rows + lax.broadcasted_iota(jnp.int32, (rows, seen), 0)
            key = lax.broadcasted_iota(jnp.int32, (rows, seen), 1)
            scores = jnp.where(key <= query, scores, -jnp.inf)
            shifted = jnp.exp(scores - jnp.max(scores, axis=1, keepdims=True))
            probs = (shifted / jnp.sum(shifted, axis=1, keepdims=True)).astype(jnp.bfloat16)
            probs_ref[h, block, :seen] = probs
            attn = dot(probs, vh[:seen, cols]).astype(jnp.bfloat16).astype(jnp.float32)
            state[block, cols] = (rh[block, cols].astype(jnp.float32) + attn).astype(jnp.bfloat16)
        if h == 0:
            pass_on(0, 1)
    for e in range(n_all):
        pack(x_send, (e,), dot(
            place_ref[e * slots:(e + 1) * slots, :], state[...]).astype(jnp.bfloat16), slots)
    start_plane(1)
    pass_on(1, 0)
    if n_context > 2:
        pass_on(0, 2)
    pass_on(1, 1)
    for away in range(3, n_context):
        pass_on(0, away)

    out_row = lax.broadcasted_iota(jnp.int32, (slots, n_context * slots), 0)
    in_row = lax.broadcasted_iota(jnp.int32, (slots, n_context * slots), 1)
    unpack = []
    for j in range(n_context):
        match = jnp.zeros((slots, n_context * slots), jnp.float32)
        for c in range(n_context):
            match = match + (
                (in_row == out_row + c * (slots - capacity) + j * capacity)
                & (out_row >= c * capacity) & (out_row < (c + 1) * capacity)).astype(jnp.float32)
        unpack.append(match)
    unpack = jnp.concatenate(unpack, axis=0).astype(jnp.bfloat16)
    for seq in range(n_expert):
        for t in range(n_tensor):
            landed = jnp.concatenate(
                [unpacked(g_land, (seq * n_tensor + t, c), slots, width)
                 for c in range(n_context)], axis=0)
            parts = dot(unpack, landed).astype(jnp.bfloat16)
            for j in range(n_context):
                at = (t * n_context + j) * width
                g_rows[seq * slots:(seq + 1) * slots, at:at + width] = parts[
                    j * slots:(j + 1) * slots]
    for away in range(2, n_context):
        pass_on(1, away)
        if away == 2:
            start_in(4)
    if n_context == 2:
        start_in(4)
    for f in range(tiles):
        part = slice(f * tile, (f + 1) * tile)
        for number in range(3):
            load(number, f).wait()
        grad_act_ref[:, part] = dot(g_rows[...], down_w[part, :], 1, 1)

    for seq in range(n_expert):
        for t in range(n_tensor):
            for c in range(n_context):
                at = (t * n_context + c) * width
                x_rows[seq * slots:(seq + 1) * slots, at:at + width] = unpacked(
                    x_land, (seq * n_tensor + t, c), slots, width)
    x32 = x_rows[...].astype(jnp.float32)
    inv_ref[...] = 1.0 / jnp.sqrt(
        jnp.sum(x32 * x32, axis=1, keepdims=True) / features + EPSILON)
    inner_ref[...] = jnp.zeros_like(inner_ref)
    for f in range(tiles):
        part = slice(f * tile, (f + 1) * tile)
        inv = inv_ref[...]
        gate = dot(x_rows[...], gate_w[:, part]) * inv
        up = dot(x_rows[...], up_w[:, part]) * inv
        grad_act = grad_act_ref[:, part]
        sig = 1.0 / (1.0 + jnp.exp(-gate))
        grad_up = grad_act * gate * sig
        grad_gate = grad_act * up * sig * (1.0 + gate * (1.0 - sig))
        act[:, part] = (gate * sig * up).astype(jnp.bfloat16)
        inner_ref[...] += jnp.sum(grad_gate * gate + grad_up * up, axis=1, keepdims=True)
        dgate[:, part] = (grad_gate * inv).astype(jnp.bfloat16)
        dup[:, part] = (grad_up * inv).astype(jnp.bfloat16)
    inner_ref[...] = inner_ref[...] * inv_ref[...] * inv_ref[...] / features

    paired = n_context == 4
    half, low = own_context // 2, lax.rem(own_context, 2)
    is_end = lax.rem(half + low + 1, 2)
    per_half = pieces // 2

    def piece_of(turn):
        if not paired:
            return turn // n_context, lax.rem(turn, n_context), False
        first = 1 - turn // per_half
        across = lax.rem(is_end + first + 1, 2)
        k = lax.rem(turn, per_half)
        context = lax.rem(half + across, 2) * 2 + lax.rem(k, 2)
        return k // 2, context, across == 1

    def piece_copy(tensor, context, seq):
        piece = tensor * n_context + context
        return remote(
            r_send.at[piece, seq], back.at[own_context, own_piece],
            back_send.at[piece, seq], back_recv.at[own_context, own_piece],
            (seq, context, tensor))

    def pair_copy(tensor, context):
        k = tensor * 2 + lax.rem(context, 2)
        return remote(
            r_send.at[tensor * n_context + context], pair_land.at[k],
            pair_send.at[k], pair_recv.at[k],
            (own_expert, own_context + 1 - 2 * half, own_tensor))

    def each_seq(tensor, context, act_on):
        @pl.loop(0, n_expert)
        def _(seq):
            @pl.when(jnp.logical_not(
                (context == own_context) & (tensor == own_tensor) & (seq == own_expert)))
            def _():
                act_on(piece_copy(tensor, context, seq))

    @pl.loop(0, pieces)
    def _(turn):
        tensor, context, across = piece_of(turn)
        piece = tensor * n_context + context
        part = aligned(piece * width, width)
        grad = dot(dgate[...], gate_w[part, :], 1, 1) + dot(dup[...], up_w[part, :], 1, 1)
        grad = grad - x_rows[:, part].astype(jnp.float32) * inner_ref[...]
        if not paired:
            for seq in range(n_expert):
                pack(r_send, (piece, seq),
                     grad[seq * slots:(seq + 1) * slots].astype(jnp.bfloat16), slots)
            each_seq(tensor, context, lambda copy: copy.start())
            return
        gather = across & (is_end == 0)

        @pl.when(jnp.logical_not(gather))
        def _():
            for seq in range(n_expert):
                pack(r_send, (piece, seq),
                     grad[seq * slots:(seq + 1) * slots].astype(jnp.bfloat16), slots)

        @pl.when(gather)
        def _():
            k = tensor * 2 + lax.rem(context, 2)
            part = pair_land.at[k]
            pltpu.make_async_copy(part, part, pair_recv.at[k]).wait()
            for seq in range(n_expert):
                both = grad[seq * slots:(seq + 1) * slots] + unpacked(
                    pair_land, (k, seq), slots, width).astype(jnp.float32)
                pack(r_send, (piece, seq), both.astype(jnp.bfloat16), slots)

        @pl.when(across & (is_end == 1))
        def _():
            pair_copy(tensor, context).start()

        @pl.when(jnp.logical_not(across & (is_end == 1)))
        def _():
            each_seq(tensor, context, lambda copy: copy.start())

    back[own_context, own_piece] = r_send[own_tensor * n_context + own_context, own_expert]

    def store(f):
        part = slice(f * tile, (f + 1) * tile)
        return pltpu.make_async_copy(
            down_out.at[part, :], down_hbm_out.at[0, part, :], store_sem.at[f])

    for f in range(tiles):
        part = slice(f * tile, (f + 1) * tile)
        down_out[part, :] = dot(act[:, part], g_rows[...], 0, 0).astype(jnp.bfloat16)
        store(f).start()
    x_turned[...] = x_rows[...].T
    chain_sent(0)
    chain_sent(1)
    arrived(4)
    for number in range(n_moves + 1):
        for step in range(1, n_context):
            in_copy(number, step).wait_send()

    sources = [half * 2, half * 2 + 1, 2 - half] if paired else list(range(n_context))

    outs = [(gr, gr_out), (gv, gv_out), (gk, gk_out), (gq, gq_out)]

    def out_copy(number, step):
        target = lax.rem(own_context + step, n_context)
        src, dst = outs[number]
        return remote(
            src.at[aligned(target * rows, rows), :],
            dst.at[:, aligned(own_context * width, width)],
            out_send.at[number, step], out_recv.at[number, step],
            (own_expert, target, own_tensor))

    def send(number):
        for step in range(1, n_context):
            out_copy(number, step).start()
        src, dst = outs[number]
        dst[:, aligned(own_context * width, width)] = src[aligned(own_context * rows, rows), :]

    change = jnp.zeros((length, width), jnp.float32)
    for source in sources:
        @pl.loop(0, n_all)
        def _(piece):
            @pl.when(jnp.logical_not((source == own_context) & (piece == own_piece)))
            def _():
                part = back.at[source, piece]
                pltpu.make_async_copy(part, part, back_recv.at[source, piece]).wait()

        landed = jnp.concatenate(
            [unpacked(back, (source, piece), slots, width) for piece in range(n_all)], axis=0)
        change = change + dot(place_ref[...], landed, 0, 0)
    gr[...] = (gh[...].astype(jnp.float32) + change).astype(jnp.bfloat16)
    send(0)
    dk_sum[...] = jnp.zeros_like(dk_sum)
    dv_sum[...] = jnp.zeros_like(dv_sum)
    for h in range(heads):
        cols = slice(h * HD, (h + 1) * HD)
        for c in range(n_context):
            seen = (c + 1) * rows
            block = slice(c * rows, seen)
            dv_sum[:seen, cols] += dot(probs_ref[h, block, :seen], gr[block, cols], 0, 0)
    gv[...] = dv_sum[...].astype(jnp.bfloat16)
    send(1)
    for h in range(heads):
        cols = slice(h * HD, (h + 1) * HD)
        for c in range(n_context):
            seen = (c + 1) * rows
            block = slice(c * rows, seen)
            probs = probs_ref[h, block, :seen].astype(jnp.float32)
            grad_probs = dot(gr[block, cols], vh[:seen, cols], 1, 1)
            row_dot = jnp.sum(probs * grad_probs, axis=1, keepdims=True)
            grad_scores = (probs * (grad_probs - row_dot) * HD ** (-0.5)).astype(jnp.bfloat16)
            gq[block, cols] = dot(grad_scores, kh[:seen, cols]).astype(jnp.bfloat16)
            dk_sum[:seen, cols] += dot(grad_scores, qh[block, cols], 0, 0)
    gk[...] = dk_sum[...].astype(jnp.bfloat16)
    send(2)
    send(3)

    @pl.loop(0, pieces)
    def _(turn):
        tensor, context, across = piece_of(turn)
        if not paired:
            each_seq(tensor, context, lambda copy: copy.wait_send())
            return

        @pl.when(across & (is_end == 1))
        def _():
            pair_copy(tensor, context).wait_send()

        @pl.when(jnp.logical_not(across & (is_end == 1)))
        def _():
            each_seq(tensor, context, lambda copy: copy.wait_send())

    for f in range(tiles):
        store(f).wait()
    for number in range(len(outs)):
        for step in range(1, n_context):
            out_copy(number, step).wait()


def finish_kernel(tile, x_hbm, dgate_hbm, dup_hbm, *refs):
    given, written = refs[:5], refs[5:10]
    grad_gate_hbm, grad_up_hbm, x_turned, dgate, dup, gate_out, up_out = refs[10:17]
    load_sem, copy_sem, store_sem = refs[17:]
    loads = [pltpu.make_async_copy(src, dst, load_sem.at[i]) for i, (src, dst) in enumerate(
        ((x_hbm, x_turned), (dgate_hbm, dgate), (dup_hbm, dup)))]
    copies = [pltpu.make_async_copy(src, dst, copy_sem.at[i])
              for i, (src, dst) in enumerate(zip(given, written))]
    for copy in loads + copies:
        copy.start()
    for copy in loads:
        copy.wait()
    stores = []
    for f in range(dgate.shape[1] // tile):
        part = slice(f * tile, (f + 1) * tile)
        for number, (rows_ref, out, hbm) in enumerate(
                ((dgate, gate_out, grad_gate_hbm), (dup, up_out, grad_up_hbm))):
            out[:, part] = dot(x_turned[...], rows_ref[:, part]).astype(jnp.bfloat16)
            stores.append(pltpu.make_async_copy(
                out.at[:, part], hbm.at[0, :, part], store_sem.at[number, f]))
            stores[-1].start()
    for copy in copies + stores:
        copy.wait()


def by_heads(queries, key_input, value_input, residual, grad_output, expert_of,
             gate_weight, up_weight, down_weight):
    rows, local = queries.shape
    n_expert, n_context, n_tensor = (
        lax.axis_size("expert"), lax.axis_size("context"), lax.axis_size("tensor"))
    sizes = (n_expert, n_context, n_tensor)
    n_all = n_expert * n_tensor
    features = local * n_tensor
    width = local // n_context
    length = rows * n_context
    hidden = gate_weight.shape[2]
    capacity = rows // n_all + max(1, rows // (8 * n_all))
    slots = capacity * n_context
    piece_rows = -(-slots * (width // LANES) // 16) * 16
    routed = n_expert * slots
    tile = min(hidden, 256)
    tiles = hidden // tile
    bf16, f32 = jnp.bfloat16, jnp.float32
    vmem = pl.BlockSpec(memory_space=pltpu.VMEM)
    hbm = pl.BlockSpec(memory_space=pl.ANY)
    dma = pltpu.SemaphoreType.DMA
    ids = jnp.broadcast_to(expert_of.reshape(1, rows), (n_all, rows))

    def shape(*dims):
        return jax.ShapeDtypeStruct(dims, bf16)

    def scratch(*dims, dtype=bf16):
        return pltpu.VMEM(dims, dtype)

    by_head = scratch(length, width)
    *small, down_grad, x_turned, dgate, dup = pl.pallas_call(
        functools.partial(layer_kernel, sizes, rows, capacity, slots, tile),
        out_shape=[shape(rows, local)] * 4
        + [shape(*down_weight.shape), shape(features, routed),
           shape(routed, hidden), shape(routed, hidden)],
        in_specs=[vmem, hbm, hbm, hbm, hbm, vmem, hbm, hbm, hbm],
        out_specs=[vmem] * 4 + [hbm] + [vmem] * 3,
        scratch_shapes=[
            by_head, by_head, by_head, by_head, by_head,
            scratch(n_context, n_all, rows, dtype=jnp.int32),
            scratch(n_all * slots, length),
            scratch(width // HD, length, length),
            by_head,
            scratch(n_all, piece_rows, LANES),
            scratch(n_all, piece_rows, LANES),
            scratch(n_all, n_context, piece_rows, LANES),
            scratch(n_all, n_context, piece_rows, LANES),
            scratch(routed, features),
            scratch(routed, features),
            scratch(features, hidden),
            scratch(features, hidden),
            scratch(hidden, features),
            scratch(routed, hidden),
            scratch(routed, hidden, dtype=f32),
            scratch(routed, 1, dtype=f32),
            scratch(routed, 1, dtype=f32),
            scratch(features // width, n_expert, piece_rows, LANES),
            scratch(n_context, n_all, piece_rows, LANES),
            scratch(2 * n_tensor, n_expert, piece_rows, LANES),
            scratch(hidden, features),
            by_head, by_head, by_head, by_head,
            scratch(length, width, dtype=f32),
            scratch(length, width, dtype=f32),
            dma((5,)), dma((6, n_context)), dma((6, n_context)),
            dma((2, n_all)), dma((2, 2, n_context, n_all)), dma((2, n_context, n_all)),
            dma((3, tiles)), dma((tiles,)),
            dma((features // width, n_expert)), dma((n_context, n_all)),
            dma((2 * n_tensor,)), dma((2 * n_tensor,)),
            dma((4, n_context)), dma((4, n_context)),
        ],
        compiler_params=pltpu.CompilerParams(
            collective_id=0, has_side_effects=True, vmem_limit_bytes=60 << 20),
    )(ids, queries, key_input, value_input, residual, grad_output,
      gate_weight, up_weight, down_weight)
    *small, down_grad, gate_grad, up_grad = pl.pallas_call(
        functools.partial(finish_kernel, tile),
        out_shape=[shape(rows, local)] * 4
        + [shape(*down_weight.shape), shape(*gate_weight.shape), shape(*up_weight.shape)],
        in_specs=[hbm] * 8,
        out_specs=[hbm] * 7,
        scratch_shapes=[
            scratch(features, routed), scratch(routed, hidden), scratch(routed, hidden),
            scratch(features, hidden), scratch(features, hidden),
            dma((3,)), dma((5,)), dma((2, tiles))],
        compiler_params=pltpu.CompilerParams(vmem_limit_bytes=60 << 20),
    )(x_turned, dgate, dup, *small, down_grad)
    return (*small, gate_grad, up_grad, down_grad)


def on_one(queries, *rest):
    if (queries.shape[1] // HD) % lax.axis_size("context") == 0:
        return by_heads(queries, *rest)
    return on_device(queries, *rest)


def solution(mesh):
    return jax.shard_map(
        on_one,
        mesh=mesh,
        in_specs=(
            P(("expert", "context"), "tensor"),
            P(("expert", "context"), "tensor"),
            P(("expert", "context"), "tensor"),
            P(("expert", "context"), "tensor"),
            P(("expert", "context"), "tensor"),
            P(("expert", "context"), None),
            P(("expert", "tensor"), None, "context"),
            P(("expert", "tensor"), None, "context"),
            P(("expert", "tensor"), "context", None),
        ),
        out_specs=(
            P(("expert", "context"), "tensor"),
            P(("expert", "context"), "tensor"),
            P(("expert", "context"), "tensor"),
            P(("expert", "context"), "tensor"),
            P(("expert", "tensor"), None, "context"),
            P(("expert", "tensor"), None, "context"),
            P(("expert", "tensor"), "context", None),
        ),
        check_vma=False,
    )
```

```python
import functools

import jax
import jax.numpy as jnp
from jax import lax
from jax.experimental import pallas as pl
from jax.experimental.pallas import tpu as pltpu
from jax.sharding import PartitionSpec as P

HD = 128
MESH = pl.DeviceIdType.MESH


EPSILON = 1e-06


def widen(array):
    return lax.optimization_barrier(array).astype(jnp.float32)


def masked_scores(query_heads, key_heads, query_start, score_scale):
    scores = (
        jnp.einsum("qhd,khd->hqk", query_heads, key_heads, preferred_element_type=jnp.float32)
        * score_scale
    )
    query_pos = query_start + jnp.arange(query_heads.shape[0], dtype=jnp.int32)
    key_pos = jnp.arange(key_heads.shape[0], dtype=jnp.int32)
    causal = key_pos[None, :] <= query_pos[:, None]
    return jnp.where(causal[None], scores, -jnp.inf)


def on_device(
    queries,
    key_input,
    value_input,
    residual,
    grad_output,
    expert_of,
    gate_weight,
    up_weight,
    down_weight,
):
    row_count = queries.shape[0]
    head_count = queries.shape[1] // HD
    n_expert = lax.axis_size("expert")
    n_tensor = lax.axis_size("tensor")
    features = queries.shape[1] * n_tensor
    score_scale = HD ** (-0.5)
    own_start = lax.axis_index("context") * row_count
    own_parity = lax.axis_index("tensor")
    all_keys, all_values = (
        lax.all_gather(key_input, "context", axis=0, tiled=True),
        lax.all_gather(value_input, "context", axis=0, tiled=True),
    )
    length = all_keys.shape[0]
    query_heads = queries.reshape(row_count, head_count, HD)
    key_heads = all_keys.reshape(length, head_count, HD)
    value_heads = all_values.reshape(length, head_count, HD)
    scores = masked_scores(query_heads, key_heads, own_start, score_scale)
    row_max = jnp.max(scores, axis=-1, keepdims=True)
    shifted = jnp.exp(scores - row_max)
    row_total = jnp.sum(shifted, axis=-1, keepdims=True)
    attn_probs = (shifted / row_total).astype(jnp.bfloat16)
    attn = jnp.einsum("hqk,khd->qhd", attn_probs, value_heads, preferred_element_type=jnp.float32)
    attn = attn.astype(jnp.bfloat16).reshape(row_count, -1)
    state = residual.astype(jnp.float32) + widen(attn)
    total_sq = lax.psum(jnp.sum(state * state, axis=-1), "tensor")
    inv_rms = (1.0 / jnp.sqrt(total_sq / features + EPSILON))[:, None]
    normed_exact = state * inv_rms
    normed = normed_exact.astype(jnp.bfloat16)
    n_all = n_expert * n_tensor
    capacity = row_count // n_all + max(1, row_count // (8 * n_all))
    expert_ids = expert_of[:, 0]
    onehot = (expert_ids[:, None] == jnp.arange(n_all, dtype=jnp.int32)[None, :]).astype(jnp.int32)
    earlier = jnp.cumsum(onehot, axis=0) - onehot
    slot_of = jnp.sum(earlier * onehot, axis=1)
    mine = expert_ids % n_tensor == own_parity
    target = jnp.where(mine, expert_ids // n_tensor * capacity + slot_of, n_expert * capacity)
    placing = (target[None, :] == jnp.arange(n_expert * capacity, dtype=jnp.int32)[:, None]).astype(
        jnp.bfloat16
    )
    full_normed, full_grad = (
        lax.all_gather(normed, "tensor", axis=1, tiled=True),
        lax.all_gather(grad_output, "tensor", axis=1, tiled=True),
    )
    send_normed = jnp.dot(placing, full_normed, preferred_element_type=jnp.float32).astype(
        jnp.bfloat16
    )
    send_grad = jnp.dot(placing, full_grad, preferred_element_type=jnp.float32).astype(jnp.bfloat16)
    send_normed = send_normed.reshape(n_expert, capacity, -1)
    send_grad = send_grad.reshape(n_expert, capacity, -1)
    got_normed, got_grad = (
        lax.all_to_all(send_normed, "expert", split_axis=0, concat_axis=0, tiled=True),
        lax.all_to_all(send_grad, "expert", split_axis=0, concat_axis=0, tiled=True),
    )
    routed_normed, routed_grad = (
        lax.all_gather(got_normed[None], "context", axis=0, tiled=True),
        lax.all_gather(got_grad[None], "context", axis=0, tiled=True),
    )
    routed_normed = routed_normed.reshape(-1, features)
    routed_grad = routed_grad.reshape(-1, features)
    gate_local = gate_weight[0]
    up_local = up_weight[0]
    down_local = down_weight[0]
    gate = jnp.dot(routed_normed, gate_local, preferred_element_type=jnp.float32)
    up_value = jnp.dot(routed_normed, up_local, preferred_element_type=jnp.float32)
    sigmoid_gate = jax.nn.sigmoid(gate)
    activation = (gate * sigmoid_gate * up_value).astype(jnp.bfloat16)
    grad_act = jnp.einsum("rd,fd->rf", routed_grad, down_local, preferred_element_type=jnp.float32)
    grad_gate_rows = (
        grad_act * up_value * sigmoid_gate * (1.0 + gate * (1.0 - sigmoid_gate))
    ).astype(jnp.bfloat16)
    grad_up_rows = (grad_act * gate * sigmoid_gate).astype(jnp.bfloat16)
    grad_down = jnp.dot(activation.T, routed_grad, preferred_element_type=jnp.float32).astype(
        jnp.bfloat16
    )[None]
    grad_gate = jnp.dot(routed_normed.T, grad_gate_rows, preferred_element_type=jnp.float32).astype(
        jnp.bfloat16
    )[None]
    grad_up = jnp.dot(routed_normed.T, grad_up_rows, preferred_element_type=jnp.float32).astype(
        jnp.bfloat16
    )[None]
    term = jnp.einsum("rf,df->rd", grad_gate_rows, gate_local, preferred_element_type=jnp.float32)
    summed_rows = lax.psum_scatter(
        term + jnp.einsum("rf,df->rd", grad_up_rows, up_local, preferred_element_type=jnp.float32),
        "context",
        scatter_dimension=0,
        tiled=True,
    )
    returned = lax.all_to_all(
        summed_rows.reshape(n_expert, capacity, -1),
        "expert",
        split_axis=0,
        concat_axis=0,
        tiled=True,
    )
    padded = jnp.concatenate(
        [returned.reshape(n_expert * capacity, -1), jnp.zeros((1, features), jnp.float32)], axis=0
    )
    full_grad_normed = jnp.take(padded, target, axis=0)
    grad_normed = lax.psum_scatter(full_grad_normed, "tensor", scatter_dimension=1, tiled=True)
    inner_sum = lax.psum(jnp.sum(normed_exact * grad_normed, axis=-1), "tensor")
    grad_state = grad_output.astype(jnp.float32) + inv_rms * (
        grad_normed - normed_exact * (inner_sum / features)[:, None]
    )
    grad_residual = grad_state.astype(jnp.bfloat16)
    grad_heads = grad_residual.reshape(row_count, head_count, HD)
    grad_probs = jnp.einsum(
        "qhd,khd->hqk", grad_heads, value_heads, preferred_element_type=jnp.float32
    )
    probs_exact = widen(attn_probs)
    row_dot = jnp.sum(probs_exact * grad_probs, axis=-1, keepdims=True)
    grad_scores = (probs_exact * (grad_probs - row_dot) * score_scale).astype(jnp.bfloat16)
    grad_queries = jnp.einsum(
        "hqk,khd->qhd", grad_scores, key_heads, preferred_element_type=jnp.float32
    )
    grad_queries = grad_queries.astype(jnp.bfloat16).reshape(row_count, -1)
    key_part = jnp.einsum(
        "hqk,qhd->khd", grad_scores, query_heads, preferred_element_type=jnp.float32
    )
    value_part = jnp.einsum(
        "hqk,qhd->khd", attn_probs, grad_heads, preferred_element_type=jnp.float32
    )
    combined = lax.psum_scatter(
        jnp.concatenate(
            [
                key_part.reshape(lax.axis_size("context") * row_count, -1),
                value_part.reshape(lax.axis_size("context") * row_count, -1),
            ],
            axis=1,
        ),
        "context",
        scatter_dimension=0,
        tiled=True,
    )
    split_at = combined.shape[1] // 2
    grad_keys = combined[:, :split_at].astype(jnp.bfloat16)
    grad_values = combined[:, split_at:].astype(jnp.bfloat16)
    return (grad_queries, grad_keys, grad_values, grad_residual, grad_gate, grad_up, grad_down)


LANES = 128


def remote(src, dst, send_sem, recv_sem, target):
    return pltpu.make_async_remote_copy(
        src_ref=src,
        dst_ref=dst,
        send_sem=send_sem,
        recv_sem=recv_sem,
        device_id=target,
        device_id_type=MESH,
    )


def position():
    return lax.axis_index("expert"), lax.axis_index("context"), lax.axis_index("tensor")


def greet_all(sizes):
    n_expert, n_context, n_tensor = sizes
    n_devices = n_expert * n_context * n_tensor
    own_expert, own_context, own_tensor = position()
    own = (own_expert * n_context + own_context) * n_tensor + own_tensor
    barrier = pltpu.get_barrier_semaphore()

    @pl.loop(1, n_devices)
    def _(step):
        other = lax.rem(own + step, n_devices)
        target = (
            other // (n_context * n_tensor),
            lax.rem(other // n_tensor, n_context),
            lax.rem(other, n_tensor),
        )
        pl.semaphore_signal(barrier, inc=1, device_id=target, device_id_type=MESH)

    return barrier, n_devices - 1


def aligned(start, size):
    return pl.ds(pl.multiple_of(start, size), size)


def dot(left, right, left_dim=1, right_dim=0):
    return lax.dot_general(
        left, right, (((left_dim,), (right_dim,)), ((), ())), preferred_element_type=jnp.float32
    )


def as_bf16(mask):
    return mask.astype(jnp.float32).astype(jnp.bfloat16)


def pack(ref, at, value, rows):
    for b in range(value.shape[1] // LANES):
        ref[(*at, slice(b * rows, (b + 1) * rows), slice(None))] = value[
            :, b * LANES:(b + 1) * LANES]


def unpacked(ref, at, rows, width):
    return jnp.concatenate(
        [ref[(*at, slice(b * rows, (b + 1) * rows), slice(None))]
         for b in range(width // LANES)], axis=1)


def layer_kernel(sizes, rows, capacity, slots, tile,
                 ids_ref, q_ref, k_ref, v_ref, r_ref, g_ref, gate_hbm, up_hbm, down_hbm,
                 gq_out, gk_out, gv_out, gr_out, down_hbm_out, x_turned, dgate, dup,
                 qh, kh, vh, rh, gh, ids_all, place_ref, probs_ref, state,
                 x_send, g_send, x_land, g_land, x_rows, g_rows,
                 gate_w, up_w, down_w, act, grad_act_ref, gate_sum, up_sum, inv_ref, inner_ref, r_send, back, pair_land,
                 down_out, gq, gk, gv, gr, dk_sum, dv_sum,
                 own_sem, in_send, in_recv, plane_send, chain_send, land_recv,
                 load_sem, store_sem, back_send, back_recv, pair_send, pair_recv, out_send, out_recv):
    n_expert, n_context, n_tensor = sizes
    n_all = n_expert * n_tensor
    own_expert, own_context, own_tensor = position()
    own_piece = own_expert * n_tensor + own_tensor
    length, width = qh.shape
    heads = width // HD
    features, hidden = gate_w.shape
    tiles = hidden // tile
    pieces = features // width
    barrier, count = greet_all(sizes)

    def load(number, f):
        part = slice(f * tile, (f + 1) * tile)
        src, dst = ((gate_hbm.at[0, :, part], gate_w.at[:, part]),
                    (up_hbm.at[0, :, part], up_w.at[:, part]),
                    (down_hbm.at[0, part, :], down_w.at[part, :]))[number]
        return pltpu.make_async_copy(src, dst, load_sem.at[number, f])

    moves = [(q_ref, qh), (k_ref, kh), (v_ref, vh), (r_ref, rh), (g_ref, gh)]
    n_moves = len(moves)

    def own_copy(number):
        src, dst = moves[number]
        return pltpu.make_async_copy(
            src.at[:, aligned(own_context * width, width)],
            dst.at[aligned(own_context * rows, rows), :], own_sem.at[number])

    for number in range(n_moves):
        own_copy(number).start()
    ids_all[own_context] = ids_ref[...]

    def in_copy(number, step):
        target = lax.rem(own_context + step, n_context)
        if number == n_moves:
            src, dst = ids_ref, ids_all.at[own_context]
        else:
            src = moves[number][0].at[:, aligned(target * width, width)]
            dst = moves[number][1].at[aligned(own_context * rows, rows), :]
        return remote(src, dst, in_send.at[number, step], in_recv.at[number, step],
                      (own_expert, target, own_tensor))

    def start_in(number):
        for step in range(1, n_context):
            in_copy(number, step).start()

    def arrived(number):
        for step in range(1, n_context):
            in_copy(number, step).wait_recv()
        if number < n_moves:
            own_copy(number).wait()

    def land(kind, plane, piece):
        return (g_land, x_land)[kind].at[piece, plane]

    def plane_copy(kind, step):
        other = lax.rem(own_piece + step, n_all)
        src = (g_send, x_send)[kind]
        return remote(
            src.at[other], land(kind, own_context, own_piece),
            plane_send.at[kind, step], land_recv.at[kind, own_context, own_piece],
            (other // n_tensor, own_context, lax.rem(other, n_tensor)))

    def chain_copy(kind, plane, piece, side):
        part = land(kind, plane, piece)
        return remote(
            part, part, chain_send.at[kind, side, plane, piece], land_recv.at[kind, plane, piece],
            (own_expert, own_context + (1, -1)[side], own_tensor))

    def await_land(kind, plane, piece):
        part = land(kind, plane, piece)
        pltpu.make_async_copy(part, part, land_recv.at[kind, plane, piece]).wait()

    has = (own_context < n_context - 1, own_context > 0)

    def start_plane(kind):
        @pl.loop(1, n_all)
        def _(step):
            plane_copy(kind, step).start()

        (g_land, x_land)[kind][own_piece, own_context] = (g_send, x_send)[kind][own_piece]

    def pass_on(kind, away):
        if away == 0:
            @pl.loop(0, n_all)
            def _(turn):
                piece = lax.rem(own_piece + turn, n_all)

                @pl.when(piece != own_piece)
                def _():
                    await_land(kind, own_context, piece)

                for side in (0, 1):
                    @pl.when(has[side])
                    def _():
                        chain_copy(kind, own_context, piece, side).start()
            return
        for side in (0, 1):
            plane = own_context + (-away, away)[side]

            @pl.when((plane >= 0) & (plane < n_context))
            def _():
                @pl.loop(0, n_all)
                def _(piece):
                    await_land(kind, plane, piece)

                    @pl.when(has[side])
                    def _():
                        chain_copy(kind, plane, piece, side).start()

    def chain_sent(kind):
        @pl.loop(1, n_all)
        def _(step):
            plane_copy(kind, step).wait_send()

        for away in range(n_context - 1):
            for side in (0, 1):
                plane = own_context + (-away, away)[side]

                @pl.when((plane >= 0) & (plane < n_context) & has[side])
                def _():
                    @pl.loop(0, n_all)
                    def _(piece):
                        chain_copy(kind, plane, piece, side).wait_send()

    named = lax.broadcasted_iota(jnp.int32, (n_all, rows), 0)
    before = as_bf16(lax.broadcasted_iota(jnp.int32, (rows, rows), 0)
                     < lax.broadcasted_iota(jnp.int32, (rows, rows), 1))
    slot = lax.broadcasted_iota(jnp.int32, (slots, rows), 0).astype(jnp.float32)

    def ranks(ids):
        onehot = (ids == named).astype(jnp.float32)
        return jnp.where(onehot > 0.5, dot(onehot.astype(jnp.bfloat16), before), -2.0 * slots)

    own_rank = ranks(ids_ref[...])
    pl.semaphore_wait(barrier, count)
    for number in (n_moves, 0, 1, 2, 3):
        start_in(number)
    for f in range(tiles):
        for number in (2, 0, 1):
            load(number, f).start()
    for e in range(n_all):
        packed = jnp.zeros((slots, width), jnp.float32)
        for j in range(n_context):
            place = as_bf16(own_rank[e:e + 1, :] + j * capacity == slot)
            packed = packed + dot(place, g_ref[:, j * width:(j + 1) * width])
        pack(g_send, (e,), packed.astype(jnp.bfloat16), slots)
    start_plane(0)
    arrived(n_moves)
    for c in range(n_context):
        rank = ranks(ids_all[c])
        for e in range(n_all):
            place_ref[e * slots:(e + 1) * slots, c * rows:(c + 1) * rows] = as_bf16(
                rank[e:e + 1, :] + c * capacity == slot)
    pass_on(0, 0)
    for number in range(4):
        arrived(number)
    for h in range(heads):
        cols = slice(h * HD, (h + 1) * HD)
        for c in range(n_context):
            seen = (c + 1) * rows
            block = slice(c * rows, seen)
            scores = dot(qh[block, cols], kh[:seen, cols], 1, 1) * HD ** (-0.5)
            query = c * rows + lax.broadcasted_iota(jnp.int32, (rows, seen), 0)
            key = lax.broadcasted_iota(jnp.int32, (rows, seen), 1)
            scores = jnp.where(key <= query, scores, -jnp.inf)
            shifted = jnp.exp(scores - jnp.max(scores, axis=1, keepdims=True))
            probs = (shifted / jnp.sum(shifted, axis=1, keepdims=True)).astype(jnp.bfloat16)
            probs_ref[h, block, :seen] = probs
            attn = dot(probs, vh[:seen, cols]).astype(jnp.bfloat16).astype(jnp.float32)
            state[block, cols] = (rh[block, cols].astype(jnp.float32) + attn).astype(jnp.bfloat16)
        if h == 0:
            pass_on(0, 1)
    for e in range(n_all):
        pack(x_send, (e,), dot(
            place_ref[e * slots:(e + 1) * slots, :], state[...]).astype(jnp.bfloat16), slots)
    start_plane(1)
    pass_on(1, 0)
    if n_context > 2:
        pass_on(0, 2)
    pass_on(1, 1)
    for away in range(3, n_context):
        pass_on(0, away)

    out_row = lax.broadcasted_iota(jnp.int32, (slots, n_context * slots), 0)
    in_row = lax.broadcasted_iota(jnp.int32, (slots, n_context * slots), 1)
    unpack = []
    for j in range(n_context):
        match = jnp.zeros((slots, n_context * slots), jnp.float32)
        for c in range(n_context):
            match = match + (
                (in_row == out_row + c * (slots - capacity) + j * capacity)
                & (out_row >= c * capacity) & (out_row < (c + 1) * capacity)).astype(jnp.float32)
        unpack.append(match)
    unpack = jnp.concatenate(unpack, axis=0).astype(jnp.bfloat16)
    for seq in range(n_expert):
        for t in range(n_tensor):
            landed = jnp.concatenate(
                [unpacked(g_land, (seq * n_tensor + t, c), slots, width)
                 for c in range(n_context)], axis=0)
            parts = dot(unpack, landed).astype(jnp.bfloat16)
            for j in range(n_context):
                at = (t * n_context + j) * width
                g_rows[seq * slots:(seq + 1) * slots, at:at + width] = parts[
                    j * slots:(j + 1) * slots]
    def absorb(plane, first=False):
        gate = jnp.zeros((n_expert * slots, hidden), jnp.float32)
        up = gate
        squares = jnp.zeros((n_expert * slots, 1), jnp.float32)
        for t in range(n_tensor):
            part = aligned((t * n_context + plane) * width, width)
            slab = jnp.concatenate(
                [unpacked(x_land, (seq * n_tensor + t, plane), slots, width)
                 for seq in range(n_expert)], axis=0)
            x_rows[:, part] = slab
            gate = gate + dot(slab, gate_w[part, :])
            up = up + dot(slab, up_w[part, :])
            wide = slab.astype(jnp.float32)
            squares = squares + jnp.sum(wide * wide, axis=1, keepdims=True)
        gate_sum[...] = gate if first else gate_sum[...] + gate
        up_sum[...] = up if first else up_sum[...] + up
        inv_ref[...] = squares if first else inv_ref[...] + squares

    def absorb_at(away):
        for plane in (own_context - away, own_context + away):
            @pl.when((plane >= 0) & (plane < n_context))
            def _():
                absorb(plane)

    for f in range(tiles):
        for number in range(3):
            load(number, f).wait()
    if n_context > 2:
        pass_on(1, 2)
    start_in(4)
    absorb(own_context, True)
    absorb_at(1)
    for f in range(tiles):
        part = slice(f * tile, (f + 1) * tile)
        grad_act_ref[:, part] = dot(g_rows[...], down_w[part, :], 1, 1)
    for away in range(2, n_context):
        absorb_at(away)
        if away + 1 < n_context:
            pass_on(1, away + 1)

    inv_ref[...] = 1.0 / jnp.sqrt(inv_ref[...] / features + EPSILON)
    inner_ref[...] = jnp.zeros_like(inner_ref)
    for f in range(tiles):
        part = slice(f * tile, (f + 1) * tile)
        inv = inv_ref[...]
        gate = gate_sum[:, part] * inv
        up = up_sum[:, part] * inv
        grad_act = grad_act_ref[:, part]
        sig = 1.0 / (1.0 + jnp.exp(-gate))
        grad_up = grad_act * gate * sig
        grad_gate = grad_act * up * sig * (1.0 + gate * (1.0 - sig))
        act[:, part] = (gate * sig * up).astype(jnp.bfloat16)
        inner_ref[...] += jnp.sum(grad_gate * gate + grad_up * up, axis=1, keepdims=True)
        dgate[:, part] = (grad_gate * inv).astype(jnp.bfloat16)
        dup[:, part] = (grad_up * inv).astype(jnp.bfloat16)
    inner_ref[...] = inner_ref[...] * inv_ref[...] * inv_ref[...] / features

    paired = n_context == 4
    half, low = own_context // 2, lax.rem(own_context, 2)
    is_end = lax.rem(half + low + 1, 2)
    per_half = pieces // 2

    def piece_of(turn):
        if not paired:
            return turn // n_context, lax.rem(turn, n_context), False
        first = 1 - turn // per_half
        across = lax.rem(is_end + first + 1, 2)
        k = lax.rem(turn, per_half)
        context = lax.rem(half + across, 2) * 2 + lax.rem(k, 2)
        return k // 2, context, across == 1

    def piece_copy(tensor, context, seq):
        piece = tensor * n_context + context
        return remote(
            r_send.at[piece, seq], back.at[own_context, own_piece],
            back_send.at[piece, seq], back_recv.at[own_context, own_piece],
            (seq, context, tensor))

    def pair_copy(tensor, context):
        k = tensor * 2 + lax.rem(context, 2)
        return remote(
            r_send.at[tensor * n_context + context], pair_land.at[k],
            pair_send.at[k], pair_recv.at[k],
            (own_expert, own_context + 1 - 2 * half, own_tensor))

    def each_seq(tensor, context, act_on):
        @pl.loop(0, n_expert)
        def _(seq):
            @pl.when(jnp.logical_not(
                (context == own_context) & (tensor == own_tensor) & (seq == own_expert)))
            def _():
                act_on(piece_copy(tensor, context, seq))

    @pl.loop(0, pieces)
    def _(turn):
        tensor, context, across = piece_of(turn)
        piece = tensor * n_context + context
        part = aligned(piece * width, width)
        grad = dot(dgate[...], gate_w[part, :], 1, 1) + dot(dup[...], up_w[part, :], 1, 1)
        grad = grad - x_rows[:, part].astype(jnp.float32) * inner_ref[...]
        if not paired:
            for seq in range(n_expert):
                pack(r_send, (piece, seq),
                     grad[seq * slots:(seq + 1) * slots].astype(jnp.bfloat16), slots)
            each_seq(tensor, context, lambda copy: copy.start())
            return
        gather = across & (is_end == 0)

        @pl.when(jnp.logical_not(gather))
        def _():
            for seq in range(n_expert):
                pack(r_send, (piece, seq),
                     grad[seq * slots:(seq + 1) * slots].astype(jnp.bfloat16), slots)

        @pl.when(gather)
        def _():
            k = tensor * 2 + lax.rem(context, 2)
            part = pair_land.at[k]
            pltpu.make_async_copy(part, part, pair_recv.at[k]).wait()
            for seq in range(n_expert):
                both = grad[seq * slots:(seq + 1) * slots] + unpacked(
                    pair_land, (k, seq), slots, width).astype(jnp.float32)
                pack(r_send, (piece, seq), both.astype(jnp.bfloat16), slots)

        @pl.when(across & (is_end == 1))
        def _():
            pair_copy(tensor, context).start()

        @pl.when(jnp.logical_not(across & (is_end == 1)))
        def _():
            each_seq(tensor, context, lambda copy: copy.start())

    back[own_context, own_piece] = r_send[own_tensor * n_context + own_context, own_expert]

    def store(f):
        part = slice(f * tile, (f + 1) * tile)
        return pltpu.make_async_copy(
            down_out.at[part, :], down_hbm_out.at[0, part, :], store_sem.at[f])

    for f in range(tiles):
        part = slice(f * tile, (f + 1) * tile)
        down_out[part, :] = dot(act[:, part], g_rows[...], 0, 0).astype(jnp.bfloat16)
        store(f).start()
    x_turned[...] = x_rows[...].T
    chain_sent(0)
    chain_sent(1)
    arrived(4)
    for number in range(n_moves + 1):
        for step in range(1, n_context):
            in_copy(number, step).wait_send()

    sources = [half * 2, half * 2 + 1, 2 - half] if paired else list(range(n_context))

    outs = [(gr, gr_out), (gv, gv_out), (gk, gk_out), (gq, gq_out)]

    def out_copy(number, step):
        target = lax.rem(own_context + step, n_context)
        src, dst = outs[number]
        return remote(
            src.at[aligned(target * rows, rows), :],
            dst.at[:, aligned(own_context * width, width)],
            out_send.at[number, step], out_recv.at[number, step],
            (own_expert, target, own_tensor))

    def send(number):
        for step in range(1, n_context):
            out_copy(number, step).start()
        src, dst = outs[number]
        dst[:, aligned(own_context * width, width)] = src[aligned(own_context * rows, rows), :]

    change = jnp.zeros((length, width), jnp.float32)
    for source in sources:
        @pl.loop(0, n_all)
        def _(piece):
            @pl.when(jnp.logical_not((source == own_context) & (piece == own_piece)))
            def _():
                part = back.at[source, piece]
                pltpu.make_async_copy(part, part, back_recv.at[source, piece]).wait()

        landed = jnp.concatenate(
            [unpacked(back, (source, piece), slots, width) for piece in range(n_all)], axis=0)
        change = change + dot(place_ref[...], landed, 0, 0)
    gr[...] = (gh[...].astype(jnp.float32) + change).astype(jnp.bfloat16)
    send(0)
    dk_sum[...] = jnp.zeros_like(dk_sum)
    dv_sum[...] = jnp.zeros_like(dv_sum)
    for h in range(heads):
        cols = slice(h * HD, (h + 1) * HD)
        for c in range(n_context):
            seen = (c + 1) * rows
            block = slice(c * rows, seen)
            dv_sum[:seen, cols] += dot(probs_ref[h, block, :seen], gr[block, cols], 0, 0)
    gv[...] = dv_sum[...].astype(jnp.bfloat16)
    send(1)
    for h in range(heads):
        cols = slice(h * HD, (h + 1) * HD)
        for c in range(n_context):
            seen = (c + 1) * rows
            block = slice(c * rows, seen)
            probs = probs_ref[h, block, :seen].astype(jnp.float32)
            grad_probs = dot(gr[block, cols], vh[:seen, cols], 1, 1)
            row_dot = jnp.sum(probs * grad_probs, axis=1, keepdims=True)
            grad_scores = (probs * (grad_probs - row_dot) * HD ** (-0.5)).astype(jnp.bfloat16)
            gq[block, cols] = dot(grad_scores, kh[:seen, cols]).astype(jnp.bfloat16)
            dk_sum[:seen, cols] += dot(grad_scores, qh[block, cols], 0, 0)
    gk[...] = dk_sum[...].astype(jnp.bfloat16)
    send(2)
    send(3)

    @pl.loop(0, pieces)
    def _(turn):
        tensor, context, across = piece_of(turn)
        if not paired:
            each_seq(tensor, context, lambda copy: copy.wait_send())
            return

        @pl.when(across & (is_end == 1))
        def _():
            pair_copy(tensor, context).wait_send()

        @pl.when(jnp.logical_not(across & (is_end == 1)))
        def _():
            each_seq(tensor, context, lambda copy: copy.wait_send())

    for f in range(tiles):
        store(f).wait()
    for number in range(len(outs)):
        for step in range(1, n_context):
            out_copy(number, step).wait()


def finish_kernel(tile, x_hbm, dgate_hbm, dup_hbm, *refs):
    given, written = refs[:5], refs[5:10]
    grad_gate_hbm, grad_up_hbm, x_turned, dgate, dup, gate_out, up_out = refs[10:17]
    held, (load_sem, in_sem, out_sem, store_sem) = refs[17:22], refs[22:]
    loads = [pltpu.make_async_copy(src, dst, load_sem.at[i]) for i, (src, dst) in enumerate(
        ((x_hbm, x_turned), (dgate_hbm, dgate), (dup_hbm, dup)))]
    ins = [pltpu.make_async_copy(src, dst, in_sem.at[i])
           for i, (src, dst) in enumerate(zip(given, held))]
    outs = [pltpu.make_async_copy(src, dst, out_sem.at[i])
            for i, (src, dst) in enumerate(zip(held, written))]
    for copy in loads + ins:
        copy.start()
    for copy in loads:
        copy.wait()
    tiles = dgate.shape[1] // tile
    for f in range(tiles):
        part = slice(f * tile, (f + 1) * tile)
        for number, (rows_ref, out, hbm) in enumerate(
                ((dgate, gate_out, grad_gate_hbm), (dup, up_out, grad_up_hbm))):
            out[:, part] = dot(x_turned[...], rows_ref[:, part]).astype(jnp.bfloat16)
            outs.append(pltpu.make_async_copy(
                out.at[:, part], hbm.at[0, :, part], store_sem.at[number, f]))
            outs[-1].start()
        if f == 0:
            for i, copy in enumerate(ins):
                copy.wait()
                outs[i].start()
    for copy in outs:
        copy.wait()


def by_heads(queries, key_input, value_input, residual, grad_output, expert_of,
             gate_weight, up_weight, down_weight):
    rows, local = queries.shape
    n_expert, n_context, n_tensor = (
        lax.axis_size("expert"), lax.axis_size("context"), lax.axis_size("tensor"))
    sizes = (n_expert, n_context, n_tensor)
    n_all = n_expert * n_tensor
    features = local * n_tensor
    width = local // n_context
    length = rows * n_context
    hidden = gate_weight.shape[2]
    capacity = rows // n_all + max(1, rows // (8 * n_all))
    slots = capacity * n_context
    piece_rows = -(-slots * (width // LANES) // 16) * 16
    routed = n_expert * slots
    tile = min(hidden, 256)
    tiles = hidden // tile
    bf16, f32 = jnp.bfloat16, jnp.float32
    vmem = pl.BlockSpec(memory_space=pltpu.VMEM)
    hbm = pl.BlockSpec(memory_space=pl.ANY)
    dma = pltpu.SemaphoreType.DMA
    ids = jnp.broadcast_to(expert_of.reshape(1, rows), (n_all, rows))

    def shape(*dims):
        return jax.ShapeDtypeStruct(dims, bf16)

    def scratch(*dims, dtype=bf16):
        return pltpu.VMEM(dims, dtype)

    by_head = scratch(length, width)
    *small, down_grad, x_turned, dgate, dup = pl.pallas_call(
        functools.partial(layer_kernel, sizes, rows, capacity, slots, tile),
        out_shape=[shape(rows, local)] * 4
        + [shape(*down_weight.shape), shape(features, routed),
           shape(routed, hidden), shape(routed, hidden)],
        in_specs=[vmem, hbm, hbm, hbm, hbm, vmem, hbm, hbm, hbm],
        out_specs=[vmem] * 4 + [hbm] + [vmem] * 3,
        scratch_shapes=[
            by_head, by_head, by_head, by_head, by_head,
            scratch(n_context, n_all, rows, dtype=jnp.int32),
            scratch(n_all * slots, length),
            scratch(width // HD, length, length),
            by_head,
            scratch(n_all, piece_rows, LANES),
            scratch(n_all, piece_rows, LANES),
            scratch(n_all, n_context, piece_rows, LANES),
            scratch(n_all, n_context, piece_rows, LANES),
            scratch(routed, features),
            scratch(routed, features),
            scratch(features, hidden),
            scratch(features, hidden),
            scratch(hidden, features),
            scratch(routed, hidden),
            scratch(routed, hidden, dtype=f32),
            scratch(routed, hidden, dtype=f32),
            scratch(routed, hidden, dtype=f32),
            scratch(routed, 1, dtype=f32),
            scratch(routed, 1, dtype=f32),
            scratch(features // width, n_expert, piece_rows, LANES),
            scratch(n_context, n_all, piece_rows, LANES),
            scratch(2 * n_tensor, n_expert, piece_rows, LANES),
            scratch(hidden, features),
            by_head, by_head, by_head, by_head,
            scratch(length, width, dtype=f32),
            scratch(length, width, dtype=f32),
            dma((5,)), dma((6, n_context)), dma((6, n_context)),
            dma((2, n_all)), dma((2, 2, n_context, n_all)), dma((2, n_context, n_all)),
            dma((3, tiles)), dma((tiles,)),
            dma((features // width, n_expert)), dma((n_context, n_all)),
            dma((2 * n_tensor,)), dma((2 * n_tensor,)),
            dma((4, n_context)), dma((4, n_context)),
        ],
        compiler_params=pltpu.CompilerParams(
            collective_id=0, has_side_effects=True, vmem_limit_bytes=60 << 20),
    )(ids, queries, key_input, value_input, residual, grad_output,
      gate_weight, up_weight, down_weight)
    *small, down_grad, gate_grad, up_grad = pl.pallas_call(
        functools.partial(finish_kernel, tile),
        out_shape=[shape(rows, local)] * 4
        + [shape(*down_weight.shape), shape(*gate_weight.shape), shape(*up_weight.shape)],
        in_specs=[hbm] * 8,
        out_specs=[hbm] * 7,
        scratch_shapes=[
            scratch(features, routed), scratch(routed, hidden), scratch(routed, hidden),
            scratch(features, hidden), scratch(features, hidden),
            *[scratch(rows, local)] * 4, scratch(*down_weight.shape),
            dma((3,)), dma((5,)), dma((5,)), dma((2, tiles))],
        compiler_params=pltpu.CompilerParams(vmem_limit_bytes=60 << 20),
    )(x_turned, dgate, dup, *small, down_grad)
    return (*small, gate_grad, up_grad, down_grad)


def on_one(queries, *rest):
    if (queries.shape[1] // HD) % lax.axis_size("context") == 0:
        return by_heads(queries, *rest)
    return on_device(queries, *rest)


def solution(mesh):
    return jax.shard_map(
        on_one,
        mesh=mesh,
        in_specs=(
            P(("expert", "context"), "tensor"),
            P(("expert", "context"), "tensor"),
            P(("expert", "context"), "tensor"),
            P(("expert", "context"), "tensor"),
            P(("expert", "context"), "tensor"),
            P(("expert", "context"), None),
            P(("expert", "tensor"), None, "context"),
            P(("expert", "tensor"), None, "context"),
            P(("expert", "tensor"), "context", None),
        ),
        out_specs=(
            P(("expert", "context"), "tensor"),
            P(("expert", "context"), "tensor"),
            P(("expert", "context"), "tensor"),
            P(("expert", "context"), "tensor"),
            P(("expert", "tensor"), None, "context"),
            P(("expert", "tensor"), None, "context"),
            P(("expert", "tensor"), "context", None),
        ),
        check_vma=False,
    )
```

```python
import functools

import jax
import jax.numpy as jnp
from jax import lax
from jax.experimental import pallas as pl
from jax.experimental.pallas import tpu as pltpu
from jax.sharding import PartitionSpec as P

HD = 128
MESH = pl.DeviceIdType.MESH


EPSILON = 1e-06


def widen(array):
    return lax.optimization_barrier(array).astype(jnp.float32)


def masked_scores(query_heads, key_heads, query_start, score_scale):
    scores = (
        jnp.einsum("qhd,khd->hqk", query_heads, key_heads, preferred_element_type=jnp.float32)
        * score_scale
    )
    query_pos = query_start + jnp.arange(query_heads.shape[0], dtype=jnp.int32)
    key_pos = jnp.arange(key_heads.shape[0], dtype=jnp.int32)
    causal = key_pos[None, :] <= query_pos[:, None]
    return jnp.where(causal[None], scores, -jnp.inf)


def on_device(
    queries,
    key_input,
    value_input,
    residual,
    grad_output,
    expert_of,
    gate_weight,
    up_weight,
    down_weight,
):
    row_count = queries.shape[0]
    head_count = queries.shape[1] // HD
    n_expert = lax.axis_size("expert")
    n_tensor = lax.axis_size("tensor")
    features = queries.shape[1] * n_tensor
    score_scale = HD ** (-0.5)
    own_start = lax.axis_index("context") * row_count
    own_parity = lax.axis_index("tensor")
    all_keys, all_values = (
        lax.all_gather(key_input, "context", axis=0, tiled=True),
        lax.all_gather(value_input, "context", axis=0, tiled=True),
    )
    length = all_keys.shape[0]
    query_heads = queries.reshape(row_count, head_count, HD)
    key_heads = all_keys.reshape(length, head_count, HD)
    value_heads = all_values.reshape(length, head_count, HD)
    scores = masked_scores(query_heads, key_heads, own_start, score_scale)
    row_max = jnp.max(scores, axis=-1, keepdims=True)
    shifted = jnp.exp(scores - row_max)
    row_total = jnp.sum(shifted, axis=-1, keepdims=True)
    attn_probs = (shifted / row_total).astype(jnp.bfloat16)
    attn = jnp.einsum("hqk,khd->qhd", attn_probs, value_heads, preferred_element_type=jnp.float32)
    attn = attn.astype(jnp.bfloat16).reshape(row_count, -1)
    state = residual.astype(jnp.float32) + widen(attn)
    total_sq = lax.psum(jnp.sum(state * state, axis=-1), "tensor")
    inv_rms = (1.0 / jnp.sqrt(total_sq / features + EPSILON))[:, None]
    normed_exact = state * inv_rms
    normed = normed_exact.astype(jnp.bfloat16)
    n_all = n_expert * n_tensor
    capacity = row_count // n_all + max(1, row_count // (8 * n_all))
    expert_ids = expert_of[:, 0]
    onehot = (expert_ids[:, None] == jnp.arange(n_all, dtype=jnp.int32)[None, :]).astype(jnp.int32)
    earlier = jnp.cumsum(onehot, axis=0) - onehot
    slot_of = jnp.sum(earlier * onehot, axis=1)
    mine = expert_ids % n_tensor == own_parity
    target = jnp.where(mine, expert_ids // n_tensor * capacity + slot_of, n_expert * capacity)
    placing = (target[None, :] == jnp.arange(n_expert * capacity, dtype=jnp.int32)[:, None]).astype(
        jnp.bfloat16
    )
    full_normed, full_grad = (
        lax.all_gather(normed, "tensor", axis=1, tiled=True),
        lax.all_gather(grad_output, "tensor", axis=1, tiled=True),
    )
    send_normed = jnp.dot(placing, full_normed, preferred_element_type=jnp.float32).astype(
        jnp.bfloat16
    )
    send_grad = jnp.dot(placing, full_grad, preferred_element_type=jnp.float32).astype(jnp.bfloat16)
    send_normed = send_normed.reshape(n_expert, capacity, -1)
    send_grad = send_grad.reshape(n_expert, capacity, -1)
    got_normed, got_grad = (
        lax.all_to_all(send_normed, "expert", split_axis=0, concat_axis=0, tiled=True),
        lax.all_to_all(send_grad, "expert", split_axis=0, concat_axis=0, tiled=True),
    )
    routed_normed, routed_grad = (
        lax.all_gather(got_normed[None], "context", axis=0, tiled=True),
        lax.all_gather(got_grad[None], "context", axis=0, tiled=True),
    )
    routed_normed = routed_normed.reshape(-1, features)
    routed_grad = routed_grad.reshape(-1, features)
    gate_local = gate_weight[0]
    up_local = up_weight[0]
    down_local = down_weight[0]
    gate = jnp.dot(routed_normed, gate_local, preferred_element_type=jnp.float32)
    up_value = jnp.dot(routed_normed, up_local, preferred_element_type=jnp.float32)
    sigmoid_gate = jax.nn.sigmoid(gate)
    activation = (gate * sigmoid_gate * up_value).astype(jnp.bfloat16)
    grad_act = jnp.einsum("rd,fd->rf", routed_grad, down_local, preferred_element_type=jnp.float32)
    grad_gate_rows = (
        grad_act * up_value * sigmoid_gate * (1.0 + gate * (1.0 - sigmoid_gate))
    ).astype(jnp.bfloat16)
    grad_up_rows = (grad_act * gate * sigmoid_gate).astype(jnp.bfloat16)
    grad_down = jnp.dot(activation.T, routed_grad, preferred_element_type=jnp.float32).astype(
        jnp.bfloat16
    )[None]
    grad_gate = jnp.dot(routed_normed.T, grad_gate_rows, preferred_element_type=jnp.float32).astype(
        jnp.bfloat16
    )[None]
    grad_up = jnp.dot(routed_normed.T, grad_up_rows, preferred_element_type=jnp.float32).astype(
        jnp.bfloat16
    )[None]
    term = jnp.einsum("rf,df->rd", grad_gate_rows, gate_local, preferred_element_type=jnp.float32)
    summed_rows = lax.psum_scatter(
        term + jnp.einsum("rf,df->rd", grad_up_rows, up_local, preferred_element_type=jnp.float32),
        "context",
        scatter_dimension=0,
        tiled=True,
    )
    returned = lax.all_to_all(
        summed_rows.reshape(n_expert, capacity, -1),
        "expert",
        split_axis=0,
        concat_axis=0,
        tiled=True,
    )
    padded = jnp.concatenate(
        [returned.reshape(n_expert * capacity, -1), jnp.zeros((1, features), jnp.float32)], axis=0
    )
    full_grad_normed = jnp.take(padded, target, axis=0)
    grad_normed = lax.psum_scatter(full_grad_normed, "tensor", scatter_dimension=1, tiled=True)
    inner_sum = lax.psum(jnp.sum(normed_exact * grad_normed, axis=-1), "tensor")
    grad_state = grad_output.astype(jnp.float32) + inv_rms * (
        grad_normed - normed_exact * (inner_sum / features)[:, None]
    )
    grad_residual = grad_state.astype(jnp.bfloat16)
    grad_heads = grad_residual.reshape(row_count, head_count, HD)
    grad_probs = jnp.einsum(
        "qhd,khd->hqk", grad_heads, value_heads, preferred_element_type=jnp.float32
    )
    probs_exact = widen(attn_probs)
    row_dot = jnp.sum(probs_exact * grad_probs, axis=-1, keepdims=True)
    grad_scores = (probs_exact * (grad_probs - row_dot) * score_scale).astype(jnp.bfloat16)
    grad_queries = jnp.einsum(
        "hqk,khd->qhd", grad_scores, key_heads, preferred_element_type=jnp.float32
    )
    grad_queries = grad_queries.astype(jnp.bfloat16).reshape(row_count, -1)
    key_part = jnp.einsum(
        "hqk,qhd->khd", grad_scores, query_heads, preferred_element_type=jnp.float32
    )
    value_part = jnp.einsum(
        "hqk,qhd->khd", attn_probs, grad_heads, preferred_element_type=jnp.float32
    )
    combined = lax.psum_scatter(
        jnp.concatenate(
            [
                key_part.reshape(lax.axis_size("context") * row_count, -1),
                value_part.reshape(lax.axis_size("context") * row_count, -1),
            ],
            axis=1,
        ),
        "context",
        scatter_dimension=0,
        tiled=True,
    )
    split_at = combined.shape[1] // 2
    grad_keys = combined[:, :split_at].astype(jnp.bfloat16)
    grad_values = combined[:, split_at:].astype(jnp.bfloat16)
    return (grad_queries, grad_keys, grad_values, grad_residual, grad_gate, grad_up, grad_down)


LANES = 128


def remote(src, dst, send_sem, recv_sem, target):
    return pltpu.make_async_remote_copy(
        src_ref=src,
        dst_ref=dst,
        send_sem=send_sem,
        recv_sem=recv_sem,
        device_id=target,
        device_id_type=MESH,
    )


def position():
    return lax.axis_index("expert"), lax.axis_index("context"), lax.axis_index("tensor")


def greet_all(sizes):
    n_expert, n_context, n_tensor = sizes
    n_devices = n_expert * n_context * n_tensor
    own_expert, own_context, own_tensor = position()
    own = (own_expert * n_context + own_context) * n_tensor + own_tensor
    barrier = pltpu.get_barrier_semaphore()

    @pl.loop(1, n_devices)
    def _(step):
        other = lax.rem(own + step, n_devices)
        target = (
            other // (n_context * n_tensor),
            lax.rem(other // n_tensor, n_context),
            lax.rem(other, n_tensor),
        )
        pl.semaphore_signal(barrier, inc=1, device_id=target, device_id_type=MESH)

    return barrier, n_devices - 1


def aligned(start, size):
    return pl.ds(pl.multiple_of(start, size), size)


def dot(left, right, left_dim=1, right_dim=0):
    return lax.dot_general(
        left, right, (((left_dim,), (right_dim,)), ((), ())), preferred_element_type=jnp.float32
    )


def as_bf16(mask):
    return mask.astype(jnp.float32).astype(jnp.bfloat16)


def pack(ref, at, value, rows):
    for b in range(value.shape[1] // LANES):
        ref[(*at, slice(b * rows, (b + 1) * rows), slice(None))] = value[
            :, b * LANES:(b + 1) * LANES]


def unpacked(ref, at, rows, width):
    return jnp.concatenate(
        [ref[(*at, slice(b * rows, (b + 1) * rows), slice(None))]
         for b in range(width // LANES)], axis=1)


def layer_kernel(sizes, rows, capacity, slots, tile,
                 ids_ref, q_ref, k_ref, v_ref, r_ref, g_ref, gate_hbm, up_hbm, down_hbm,
                 gq_out, gk_out, gv_out, gr_out, down_hbm_out, x_turned, dgate, dup,
                 qh, kh, vh, rh, gh, ids_all, place_ref, probs_ref, state,
                 x_send, g_send, x_land, g_land, x_rows, g_rows,
                 gate_w, up_w, down_w, act, grad_act_ref, gate_sum, up_sum, inv_ref, inner_ref, r_send, back, pair_land,
                 down_out, gq, gk, gv, gr, dk_sum, dv_sum,
                 own_sem, in_send, in_recv, plane_send, chain_send, land_recv,
                 load_sem, store_sem, back_send, back_recv, pair_send, pair_recv, out_send, out_recv):
    n_expert, n_context, n_tensor = sizes
    n_all = n_expert * n_tensor
    own_expert, own_context, own_tensor = position()
    own_piece = own_expert * n_tensor + own_tensor
    length, width = qh.shape
    heads = width // HD
    features, hidden = gate_w.shape
    tiles = hidden // tile
    pieces = features // width
    barrier, count = greet_all(sizes)

    def load(number, f):
        part = slice(f * tile, (f + 1) * tile)
        src, dst = ((gate_hbm.at[0, :, part], gate_w.at[:, part]),
                    (up_hbm.at[0, :, part], up_w.at[:, part]),
                    (down_hbm.at[0, part, :], down_w.at[part, :]))[number]
        return pltpu.make_async_copy(src, dst, load_sem.at[number, f])

    moves = [(q_ref, qh), (k_ref, kh), (v_ref, vh), (r_ref, rh), (g_ref, gh)]
    n_moves = len(moves)

    def own_copy(number):
        src, dst = moves[number]
        return pltpu.make_async_copy(
            src.at[:, aligned(own_context * width, width)],
            dst.at[aligned(own_context * rows, rows), :], own_sem.at[number])

    for number in range(n_moves):
        own_copy(number).start()
    ids_all[own_context] = ids_ref[...]

    def in_copy(number, step):
        target = lax.rem(own_context + step, n_context)
        if number == n_moves:
            src, dst = ids_ref, ids_all.at[own_context]
        else:
            src = moves[number][0].at[:, aligned(target * width, width)]
            dst = moves[number][1].at[aligned(own_context * rows, rows), :]
        return remote(src, dst, in_send.at[number, step], in_recv.at[number, step],
                      (own_expert, target, own_tensor))

    def start_in(number):
        for step in range(1, n_context):
            in_copy(number, step).start()

    def arrived(number):
        for step in range(1, n_context):
            in_copy(number, step).wait_recv()
        if number < n_moves:
            own_copy(number).wait()

    def land(kind, plane, piece):
        return (g_land, x_land)[kind].at[piece, plane]

    def plane_copy(kind, step):
        other = lax.rem(own_piece + step, n_all)
        src = (g_send, x_send)[kind]
        return remote(
            src.at[other], land(kind, own_context, own_piece),
            plane_send.at[kind, step], land_recv.at[kind, own_context, own_piece],
            (other // n_tensor, own_context, lax.rem(other, n_tensor)))

    def chain_copy(kind, plane, piece, side):
        part = land(kind, plane, piece)
        return remote(
            part, part, chain_send.at[kind, side, plane, piece], land_recv.at[kind, plane, piece],
            (own_expert, own_context + (1, -1)[side], own_tensor))

    def await_land(kind, plane, piece):
        part = land(kind, plane, piece)
        pltpu.make_async_copy(part, part, land_recv.at[kind, plane, piece]).wait()

    has = (own_context < n_context - 1, own_context > 0)

    def start_plane(kind):
        @pl.loop(1, n_all)
        def _(step):
            plane_copy(kind, step).start()

        (g_land, x_land)[kind][own_piece, own_context] = (g_send, x_send)[kind][own_piece]

    def pass_on(kind, away):
        if away == 0:
            @pl.loop(0, n_all)
            def _(turn):
                piece = lax.rem(own_piece + turn, n_all)

                @pl.when(piece != own_piece)
                def _():
                    await_land(kind, own_context, piece)

                for side in (0, 1):
                    @pl.when(has[side])
                    def _():
                        chain_copy(kind, own_context, piece, side).start()
            return
        for side in (0, 1):
            plane = own_context + (-away, away)[side]

            @pl.when((plane >= 0) & (plane < n_context))
            def _():
                @pl.loop(0, n_all)
                def _(piece):
                    await_land(kind, plane, piece)

                    @pl.when(has[side])
                    def _():
                        chain_copy(kind, plane, piece, side).start()

    def chain_sent(kind):
        @pl.loop(1, n_all)
        def _(step):
            plane_copy(kind, step).wait_send()

        for away in range(n_context - 1):
            for side in (0, 1):
                plane = own_context + (-away, away)[side]

                @pl.when((plane >= 0) & (plane < n_context) & has[side])
                def _():
                    @pl.loop(0, n_all)
                    def _(piece):
                        chain_copy(kind, plane, piece, side).wait_send()

    named = lax.broadcasted_iota(jnp.int32, (n_all, rows), 0)
    before = as_bf16(lax.broadcasted_iota(jnp.int32, (rows, rows), 0)
                     < lax.broadcasted_iota(jnp.int32, (rows, rows), 1))
    slot = lax.broadcasted_iota(jnp.int32, (slots, rows), 0).astype(jnp.float32)

    def ranks(ids):
        onehot = (ids == named).astype(jnp.float32)
        return jnp.where(onehot > 0.5, dot(onehot.astype(jnp.bfloat16), before), -2.0 * slots)

    own_rank = ranks(ids_ref[...])
    pl.semaphore_wait(barrier, count)
    for number in (n_moves, 0, 1, 2, 3):
        start_in(number)
    for f in range(tiles):
        for number in (2, 0, 1):
            load(number, f).start()
    for e in range(n_all):
        packed = jnp.zeros((slots, width), jnp.float32)
        for j in range(n_context):
            place = as_bf16(own_rank[e:e + 1, :] + j * capacity == slot)
            packed = packed + dot(place, g_ref[:, j * width:(j + 1) * width])
        pack(g_send, (e,), packed.astype(jnp.bfloat16), slots)
    start_plane(0)
    arrived(n_moves)
    for c in range(n_context):
        rank = ranks(ids_all[c])
        for e in range(n_all):
            place_ref[e * slots:(e + 1) * slots, c * rows:(c + 1) * rows] = as_bf16(
                rank[e:e + 1, :] + c * capacity == slot)
    pass_on(0, 0)
    for number in range(4):
        arrived(number)
    for h in range(heads):
        cols = slice(h * HD, (h + 1) * HD)
        for c in range(n_context):
            seen = (c + 1) * rows
            block = slice(c * rows, seen)
            scores = dot(qh[block, cols], kh[:seen, cols], 1, 1) * HD ** (-0.5)
            query = c * rows + lax.broadcasted_iota(jnp.int32, (rows, seen), 0)
            key = lax.broadcasted_iota(jnp.int32, (rows, seen), 1)
            scores = jnp.where(key <= query, scores, -jnp.inf)
            shifted = jnp.exp(scores - jnp.max(scores, axis=1, keepdims=True))
            probs = (shifted / jnp.sum(shifted, axis=1, keepdims=True)).astype(jnp.bfloat16)
            probs_ref[h, block, :seen] = probs
            attn = dot(probs, vh[:seen, cols]).astype(jnp.bfloat16).astype(jnp.float32)
            state[block, cols] = (rh[block, cols].astype(jnp.float32) + attn).astype(jnp.bfloat16)
        if h == 0:
            pass_on(0, 1)
    for e in range(n_all):
        pack(x_send, (e,), dot(
            place_ref[e * slots:(e + 1) * slots, :], state[...]).astype(jnp.bfloat16), slots)
    start_plane(1)
    pass_on(1, 0)
    if n_context > 2:
        pass_on(0, 2)
    pass_on(1, 1)
    for away in range(3, n_context):
        pass_on(0, away)

    out_row = lax.broadcasted_iota(jnp.int32, (slots, n_context * slots), 0)
    in_row = lax.broadcasted_iota(jnp.int32, (slots, n_context * slots), 1)
    unpack = []
    for j in range(n_context):
        match = jnp.zeros((slots, n_context * slots), jnp.float32)
        for c in range(n_context):
            match = match + (
                (in_row == out_row + c * (slots - capacity) + j * capacity)
                & (out_row >= c * capacity) & (out_row < (c + 1) * capacity)).astype(jnp.float32)
        unpack.append(match)
    unpack = jnp.concatenate(unpack, axis=0).astype(jnp.bfloat16)
    for seq in range(n_expert):
        for t in range(n_tensor):
            landed = jnp.concatenate(
                [unpacked(g_land, (seq * n_tensor + t, c), slots, width)
                 for c in range(n_context)], axis=0)
            parts = dot(unpack, landed).astype(jnp.bfloat16)
            for j in range(n_context):
                at = (t * n_context + j) * width
                g_rows[seq * slots:(seq + 1) * slots, at:at + width] = parts[
                    j * slots:(j + 1) * slots]
    def absorb(plane, first=False):
        gate = jnp.zeros((n_expert * slots, hidden), jnp.float32)
        up = gate
        squares = jnp.zeros((n_expert * slots, 1), jnp.float32)
        for t in range(n_tensor):
            part = aligned((t * n_context + plane) * width, width)
            slab = jnp.concatenate(
                [unpacked(x_land, (seq * n_tensor + t, plane), slots, width)
                 for seq in range(n_expert)], axis=0)
            x_rows[:, part] = slab
            gate = gate + dot(slab, gate_w[part, :])
            up = up + dot(slab, up_w[part, :])
            wide = slab.astype(jnp.float32)
            squares = squares + jnp.sum(wide * wide, axis=1, keepdims=True)
        gate_sum[...] = gate if first else gate_sum[...] + gate
        up_sum[...] = up if first else up_sum[...] + up
        inv_ref[...] = squares if first else inv_ref[...] + squares

    def absorb_at(away):
        for plane in (own_context - away, own_context + away):
            @pl.when((plane >= 0) & (plane < n_context))
            def _():
                absorb(plane)

    for f in range(tiles):
        for number in range(3):
            load(number, f).wait()
    absorb(own_context, True)
    if n_context > 2:
        pass_on(1, 2)
    start_in(4)
    absorb_at(1)
    for f in range(tiles):
        part = slice(f * tile, (f + 1) * tile)
        grad_act_ref[:, part] = dot(g_rows[...], down_w[part, :], 1, 1)
    for away in range(2, n_context):
        absorb_at(away)
        if away + 1 < n_context:
            pass_on(1, away + 1)

    inv_ref[...] = 1.0 / jnp.sqrt(inv_ref[...] / features + EPSILON)
    inner_ref[...] = jnp.zeros_like(inner_ref)
    for f in range(tiles):
        part = slice(f * tile, (f + 1) * tile)
        inv = inv_ref[...]
        gate = gate_sum[:, part] * inv
        up = up_sum[:, part] * inv
        grad_act = grad_act_ref[:, part]
        sig = 1.0 / (1.0 + jnp.exp(-gate))
        grad_up = grad_act * gate * sig
        grad_gate = grad_act * up * sig * (1.0 + gate * (1.0 - sig))
        act[:, part] = (gate * sig * up).astype(jnp.bfloat16)
        inner_ref[...] += jnp.sum(grad_gate * gate + grad_up * up, axis=1, keepdims=True)
        dgate[:, part] = (grad_gate * inv).astype(jnp.bfloat16)
        dup[:, part] = (grad_up * inv).astype(jnp.bfloat16)
    inner_ref[...] = inner_ref[...] * inv_ref[...] * inv_ref[...] / features

    paired = n_context == 4
    half, low = own_context // 2, lax.rem(own_context, 2)
    is_end = lax.rem(half + low + 1, 2)
    per_half = pieces // 2

    def piece_of(turn):
        if not paired:
            return turn // n_context, lax.rem(turn, n_context), False
        first = 1 - turn // per_half
        across = lax.rem(is_end + first + 1, 2)
        k = lax.rem(turn, per_half)
        context = lax.rem(half + across, 2) * 2 + lax.rem(k, 2)
        return k // 2, context, across == 1

    def piece_copy(tensor, context, seq):
        piece = tensor * n_context + context
        return remote(
            r_send.at[piece, seq], back.at[own_context, own_piece],
            back_send.at[piece, seq], back_recv.at[own_context, own_piece],
            (seq, context, tensor))

    def pair_copy(tensor, context):
        k = tensor * 2 + lax.rem(context, 2)
        return remote(
            r_send.at[tensor * n_context + context], pair_land.at[k],
            pair_send.at[k], pair_recv.at[k],
            (own_expert, own_context + 1 - 2 * half, own_tensor))

    def each_seq(tensor, context, act_on):
        @pl.loop(0, n_expert)
        def _(seq):
            @pl.when(jnp.logical_not(
                (context == own_context) & (tensor == own_tensor) & (seq == own_expert)))
            def _():
                act_on(piece_copy(tensor, context, seq))

    @pl.loop(0, pieces)
    def _(turn):
        tensor, context, across = piece_of(turn)
        piece = tensor * n_context + context
        part = aligned(piece * width, width)
        grad = dot(dgate[...], gate_w[part, :], 1, 1) + dot(dup[...], up_w[part, :], 1, 1)
        grad = grad - x_rows[:, part].astype(jnp.float32) * inner_ref[...]
        if not paired:
            for seq in range(n_expert):
                pack(r_send, (piece, seq),
                     grad[seq * slots:(seq + 1) * slots].astype(jnp.bfloat16), slots)
            each_seq(tensor, context, lambda copy: copy.start())
            return
        gather = across & (is_end == 0)

        @pl.when(jnp.logical_not(gather))
        def _():
            for seq in range(n_expert):
                pack(r_send, (piece, seq),
                     grad[seq * slots:(seq + 1) * slots].astype(jnp.bfloat16), slots)

        @pl.when(gather)
        def _():
            k = tensor * 2 + lax.rem(context, 2)
            part = pair_land.at[k]
            pltpu.make_async_copy(part, part, pair_recv.at[k]).wait()
            for seq in range(n_expert):
                both = grad[seq * slots:(seq + 1) * slots] + unpacked(
                    pair_land, (k, seq), slots, width).astype(jnp.float32)
                pack(r_send, (piece, seq), both.astype(jnp.bfloat16), slots)

        @pl.when(across & (is_end == 1))
        def _():
            pair_copy(tensor, context).start()

        @pl.when(jnp.logical_not(across & (is_end == 1)))
        def _():
            each_seq(tensor, context, lambda copy: copy.start())

    back[own_context, own_piece] = r_send[own_tensor * n_context + own_context, own_expert]

    def store(f):
        part = slice(f * tile, (f + 1) * tile)
        return pltpu.make_async_copy(
            down_out.at[part, :], down_hbm_out.at[0, part, :], store_sem.at[f])

    for f in range(tiles):
        part = slice(f * tile, (f + 1) * tile)
        down_out[part, :] = dot(act[:, part], g_rows[...], 0, 0).astype(jnp.bfloat16)
        store(f).start()
    x_turned[...] = x_rows[...].T
    chain_sent(0)
    chain_sent(1)
    arrived(4)
    for number in range(n_moves + 1):
        for step in range(1, n_context):
            in_copy(number, step).wait_send()

    sources = [half * 2, half * 2 + 1, 2 - half] if paired else list(range(n_context))

    outs = [(gr, gr_out), (gv, gv_out), (gk, gk_out), (gq, gq_out)]

    def out_copy(number, step):
        target = lax.rem(own_context + step, n_context)
        src, dst = outs[number]
        return remote(
            src.at[aligned(target * rows, rows), :],
            dst.at[:, aligned(own_context * width, width)],
            out_send.at[number, step], out_recv.at[number, step],
            (own_expert, target, own_tensor))

    def send(number):
        for step in range(1, n_context):
            out_copy(number, step).start()
        src, dst = outs[number]
        dst[:, aligned(own_context * width, width)] = src[aligned(own_context * rows, rows), :]

    change = jnp.zeros((length, width), jnp.float32)
    for source in sources:
        @pl.loop(0, n_all)
        def _(piece):
            @pl.when(jnp.logical_not((source == own_context) & (piece == own_piece)))
            def _():
                part = back.at[source, piece]
                pltpu.make_async_copy(part, part, back_recv.at[source, piece]).wait()

        landed = jnp.concatenate(
            [unpacked(back, (source, piece), slots, width) for piece in range(n_all)], axis=0)
        change = change + dot(place_ref[...], landed, 0, 0)
    gr[...] = (gh[...].astype(jnp.float32) + change).astype(jnp.bfloat16)
    send(0)
    dk_sum[...] = jnp.zeros_like(dk_sum)
    dv_sum[...] = jnp.zeros_like(dv_sum)
    for h in range(heads):
        cols = slice(h * HD, (h + 1) * HD)
        for c in range(n_context):
            seen = (c + 1) * rows
            block = slice(c * rows, seen)
            dv_sum[:seen, cols] += dot(probs_ref[h, block, :seen], gr[block, cols], 0, 0)
    gv[...] = dv_sum[...].astype(jnp.bfloat16)
    send(1)
    for h in range(heads):
        cols = slice(h * HD, (h + 1) * HD)
        for c in range(n_context):
            seen = (c + 1) * rows
            block = slice(c * rows, seen)
            probs = probs_ref[h, block, :seen].astype(jnp.float32)
            grad_probs = dot(gr[block, cols], vh[:seen, cols], 1, 1)
            row_dot = jnp.sum(probs * grad_probs, axis=1, keepdims=True)
            grad_scores = (probs * (grad_probs - row_dot) * HD ** (-0.5)).astype(jnp.bfloat16)
            gq[block, cols] = dot(grad_scores, kh[:seen, cols]).astype(jnp.bfloat16)
            dk_sum[:seen, cols] += dot(grad_scores, qh[block, cols], 0, 0)
    gk[...] = dk_sum[...].astype(jnp.bfloat16)
    send(2)
    send(3)

    @pl.loop(0, pieces)
    def _(turn):
        tensor, context, across = piece_of(turn)
        if not paired:
            each_seq(tensor, context, lambda copy: copy.wait_send())
            return

        @pl.when(across & (is_end == 1))
        def _():
            pair_copy(tensor, context).wait_send()

        @pl.when(jnp.logical_not(across & (is_end == 1)))
        def _():
            each_seq(tensor, context, lambda copy: copy.wait_send())

    for f in range(tiles):
        store(f).wait()
    for number in range(len(outs)):
        for step in range(1, n_context):
            out_copy(number, step).wait()


def finish_kernel(tile, x_hbm, dgate_hbm, dup_hbm, *refs):
    given, written = refs[:5], refs[5:10]
    grad_gate_hbm, grad_up_hbm, x_turned, dgate, dup, gate_out, up_out = refs[10:17]
    held, (load_sem, in_sem, out_sem, store_sem) = refs[17:22], refs[22:]
    loads = [pltpu.make_async_copy(src, dst, load_sem.at[i]) for i, (src, dst) in enumerate(
        ((x_hbm, x_turned), (dgate_hbm, dgate), (dup_hbm, dup)))]
    ins = [pltpu.make_async_copy(src, dst, in_sem.at[i])
           for i, (src, dst) in enumerate(zip(given, held))]
    outs = [pltpu.make_async_copy(src, dst, out_sem.at[i])
            for i, (src, dst) in enumerate(zip(held, written))]
    for copy in loads:
        copy.start()
    for copy in loads:
        copy.wait()
    for copy in ins:
        copy.start()
    tiles = dgate.shape[1] // tile
    for f in range(tiles):
        part = slice(f * tile, (f + 1) * tile)
        for number, (rows_ref, out, hbm) in enumerate(
                ((dgate, gate_out, grad_gate_hbm), (dup, up_out, grad_up_hbm))):
            out[:, part] = dot(x_turned[...], rows_ref[:, part]).astype(jnp.bfloat16)
            outs.append(pltpu.make_async_copy(
                out.at[:, part], hbm.at[0, :, part], store_sem.at[number, f]))
            outs[-1].start()
        if f == 0:
            for i, copy in enumerate(ins):
                copy.wait()
                outs[i].start()
    for copy in outs:
        copy.wait()


def by_heads(queries, key_input, value_input, residual, grad_output, expert_of,
             gate_weight, up_weight, down_weight):
    rows, local = queries.shape
    n_expert, n_context, n_tensor = (
        lax.axis_size("expert"), lax.axis_size("context"), lax.axis_size("tensor"))
    sizes = (n_expert, n_context, n_tensor)
    n_all = n_expert * n_tensor
    features = local * n_tensor
    width = local // n_context
    length = rows * n_context
    hidden = gate_weight.shape[2]
    capacity = rows // n_all + max(1, rows // (8 * n_all))
    slots = capacity * n_context
    piece_rows = -(-slots * (width // LANES) // 16) * 16
    routed = n_expert * slots
    tile = min(hidden, 256)
    tiles = hidden // tile
    bf16, f32 = jnp.bfloat16, jnp.float32
    vmem = pl.BlockSpec(memory_space=pltpu.VMEM)
    hbm = pl.BlockSpec(memory_space=pl.ANY)
    dma = pltpu.SemaphoreType.DMA
    ids = jnp.broadcast_to(expert_of.reshape(1, rows), (n_all, rows))

    def shape(*dims):
        return jax.ShapeDtypeStruct(dims, bf16)

    def scratch(*dims, dtype=bf16):
        return pltpu.VMEM(dims, dtype)

    by_head = scratch(length, width)
    *small, down_grad, x_turned, dgate, dup = pl.pallas_call(
        functools.partial(layer_kernel, sizes, rows, capacity, slots, tile),
        out_shape=[shape(rows, local)] * 4
        + [shape(*down_weight.shape), shape(features, routed),
           shape(routed, hidden), shape(routed, hidden)],
        in_specs=[vmem, hbm, hbm, hbm, hbm, vmem, hbm, hbm, hbm],
        out_specs=[vmem] * 4 + [hbm] + [vmem] * 3,
        scratch_shapes=[
            by_head, by_head, by_head, by_head, by_head,
            scratch(n_context, n_all, rows, dtype=jnp.int32),
            scratch(n_all * slots, length),
            scratch(width // HD, length, length),
            by_head,
            scratch(n_all, piece_rows, LANES),
            scratch(n_all, piece_rows, LANES),
            scratch(n_all, n_context, piece_rows, LANES),
            scratch(n_all, n_context, piece_rows, LANES),
            scratch(routed, features),
            scratch(routed, features),
            scratch(features, hidden),
            scratch(features, hidden),
            scratch(hidden, features),
            scratch(routed, hidden),
            scratch(routed, hidden, dtype=f32),
            scratch(routed, hidden, dtype=f32),
            scratch(routed, hidden, dtype=f32),
            scratch(routed, 1, dtype=f32),
            scratch(routed, 1, dtype=f32),
            scratch(features // width, n_expert, piece_rows, LANES),
            scratch(n_context, n_all, piece_rows, LANES),
            scratch(2 * n_tensor, n_expert, piece_rows, LANES),
            scratch(hidden, features),
            by_head, by_head, by_head, by_head,
            scratch(length, width, dtype=f32),
            scratch(length, width, dtype=f32),
            dma((5,)), dma((6, n_context)), dma((6, n_context)),
            dma((2, n_all)), dma((2, 2, n_context, n_all)), dma((2, n_context, n_all)),
            dma((3, tiles)), dma((tiles,)),
            dma((features // width, n_expert)), dma((n_context, n_all)),
            dma((2 * n_tensor,)), dma((2 * n_tensor,)),
            dma((4, n_context)), dma((4, n_context)),
        ],
        compiler_params=pltpu.CompilerParams(
            collective_id=0, has_side_effects=True, vmem_limit_bytes=60 << 20),
    )(ids, queries, key_input, value_input, residual, grad_output,
      gate_weight, up_weight, down_weight)
    *small, down_grad, gate_grad, up_grad = pl.pallas_call(
        functools.partial(finish_kernel, tile),
        out_shape=[shape(rows, local)] * 4
        + [shape(*down_weight.shape), shape(*gate_weight.shape), shape(*up_weight.shape)],
        in_specs=[hbm] * 8,
        out_specs=[hbm] * 7,
        scratch_shapes=[
            scratch(features, routed), scratch(routed, hidden), scratch(routed, hidden),
            scratch(features, hidden), scratch(features, hidden),
            *[scratch(rows, local)] * 4, scratch(*down_weight.shape),
            dma((3,)), dma((5,)), dma((5,)), dma((2, tiles))],
        compiler_params=pltpu.CompilerParams(vmem_limit_bytes=60 << 20),
    )(x_turned, dgate, dup, *small, down_grad)
    return (*small, gate_grad, up_grad, down_grad)


def on_one(queries, *rest):
    if (queries.shape[1] // HD) % lax.axis_size("context") == 0:
        return by_heads(queries, *rest)
    return on_device(queries, *rest)


def solution(mesh):
    return jax.shard_map(
        on_one,
        mesh=mesh,
        in_specs=(
            P(("expert", "context"), "tensor"),
            P(("expert", "context"), "tensor"),
            P(("expert", "context"), "tensor"),
            P(("expert", "context"), "tensor"),
            P(("expert", "context"), "tensor"),
            P(("expert", "context"), None),
            P(("expert", "tensor"), None, "context"),
            P(("expert", "tensor"), None, "context"),
            P(("expert", "tensor"), "context", None),
        ),
        out_specs=(
            P(("expert", "context"), "tensor"),
            P(("expert", "context"), "tensor"),
            P(("expert", "context"), "tensor"),
            P(("expert", "context"), "tensor"),
            P(("expert", "tensor"), None, "context"),
            P(("expert", "tensor"), None, "context"),
            P(("expert", "tensor"), "context", None),
        ),
        check_vma=False,
    )
```
